256 devices in a mesh: dp: 16 (over x_hi, y, core), ctx: 16 (over z, x_lo).
Axes of the slice: x: 4 (x_hi: 2, x_lo: 2; x = x_hi * 2 + x_lo), y: 4, z: 8, core: 2. Of those that a mesh axis runs over, the one named last changes fastest.
Arguments:
- queries: bfloat16 [16, 2048, 6144], P('dp', 'ctx'), may hold values from -4 to 4
- keys: bfloat16 [16, 2048, 512], P('dp', 'ctx'), may hold values from -4 to 4
- values: bfloat16 [16, 2048, 512], P('dp', 'ctx'), may hold values from -6 to 6
- saved_output: bfloat16 [16, 2048, 6144], P('dp', 'ctx'), may hold values from -6 to 6
- output_grad: bfloat16 [16, 2048, 6144], P('dp', 'ctx'), may hold values from -6 to 6
- log_sums: float32 [16, 48, 2048], P('dp', None, 'ctx'), may hold values from 0 to 12
- layer_input: bfloat16 [16, 2048, 5120], P('dp', 'ctx'), may hold values from -6 to 6
- parents: int32 [16, 16], P('dp'), may hold values from 0 to 14, as said below
- placement: int32 [16, 16], P('dp'), may hold values from 0 to 15, as said below
- tool_spans: int32 [16, 8, 2], P('dp'), may hold values from 0 to 2048, as said below
Outputs:
- query_grad: bfloat16 [16, 2048, 6144], P('dp', 'ctx')
- key_grad: bfloat16 [16, 2048, 512], P('dp', 'ctx')
- value_grad: bfloat16 [16, 2048, 512], P('dp', 'ctx')
- weight_grad: float32 [512, 5120], P(('dp', 'ctx'))
The draws below stay inside these ranges and needn't reach their ends.
Inputs may be any that keep to these rules, and one draw needn't show every extreme that they name: parents[t, 0] = 0 marks the root; for b > 0, parents[t, b] < b; the last block continues the block before it, parents[t, 15] = 14. `placement`: each row is a permutation of the 16 tree blocks. `tool_spans`: span m of a tree lies in stored positions m * 256 to (m + 1) * 256 - 1 and is not empty; the last span ends at 2048.
All inputs are finite; a program needn't handle non-finite values.
Results may differ from the reference program's by a relative error of at most 0.0051.
Values may be sent and summed in bfloat16 or wider, within the bound.
No kernel may reach another device: no remote copies, remote signals or barrier semaphores. Data moves between devices by JAX's collectives and lax.ppermute only.
A program may use at most 128 MiB of HBM per device.

```python
import math
import jax
import jax.numpy as jnp
from jax import lax

D = 5120
QH = 48
KVH = 4
DH = 128
BLOCK = 128
SPANS = 8
TREES = 16
TOKENS = 2048
BLOCKS = 16


HIGHEST = lax.Precision.HIGHEST


def tree_layouts(key):
    count = TOKENS // BLOCK
    index = jnp.arange(count, dtype=jnp.int32)

    def one_tree(tree_key):
        chain_key, pick_key, order_key = jax.random.split(tree_key, 3)
        follow = jax.random.randint(chain_key, (count,), 0, 10) < 7
        earlier = jax.random.randint(pick_key, (count,), 0, jnp.maximum(index, 1))
        parent = jnp.where(follow | (index == count - 1), index - 1, earlier)
        parent = jnp.where(index == 0, 0, parent).astype(jnp.int32)
        order = jax.random.permutation(order_key, count).astype(jnp.int32)
        return (parent, order)
    return jax.vmap(one_tree)(jax.random.split(key, TREES))


def visible_counts(parent_row, placement_row):
    count = parent_row.shape[0]
    steps = jax.nn.one_hot(parent_row, count, dtype=jnp.float32)
    identity = jnp.eye(count, dtype=jnp.float32)

    def climb(index, state):
        reach, walker = state
        walker = jnp.dot(walker, steps, precision=HIGHEST)
        return (jnp.maximum(reach, walker), walker)
    reach, walker = lax.fori_loop(0, count, climb, (identity, identity))
    placed = jax.nn.one_hot(placement_row, count, dtype=jnp.float32)
    visible = jnp.dot(jnp.dot(placed, reach, precision=HIGHEST), placed.T, precision=HIGHEST)
    return jnp.sum(visible, axis=1)


def draw_parents(key, part):
    layouts = tree_layouts(key)
    key = jax.random.fold_in(key, 2)
    return layouts[0]


def draw_placement(key, part):
    layouts = tree_layouts(key)
    key = jax.random.fold_in(key, 3)
    return layouts[1]


def draw_log_sums(key, part):
    parent_rows, placement_rows = tree_layouts(key)
    key = jax.random.fold_in(key, 4)
    others = jax.vmap(visible_counts)(parent_rows, placement_rows) - 1.0
    positions = jnp.arange(TOKENS, dtype=jnp.int32)
    within = (positions % BLOCK + 1).astype(jnp.float32)
    counts = BLOCK * jnp.repeat(others, BLOCK, axis=1) + within[None, :]
    noise = jax.random.uniform(key, (TREES, QH, TOKENS), minval=-0.25, maxval=0.25)
    return (jnp.log(counts)[:, None, :] + 0.5 + noise).astype(jnp.float32)


def draw_queries(key, part):
    key = jax.random.fold_in(key, 5)
    drawn = jnp.clip(jax.random.normal(key, (TREES, TOKENS, QH * DH)), -4.0, 4.0)
    return drawn.astype(jnp.bfloat16)


def draw_keys(key, part):
    key = jax.random.fold_in(key, 6)
    drawn = jnp.clip(jax.random.normal(key, (TREES, TOKENS, KVH * DH)), -4.0, 4.0)
    return drawn.astype(jnp.bfloat16)


def draw_tool_spans(key, part):
    key = jax.random.fold_in(key, 7)
    segment = TOKENS // SPANS
    start_key, size_key = jax.random.split(key)
    offsets = jax.random.randint(start_key, (TREES, SPANS), 0, segment // 2)
    sizes = jax.random.randint(size_key, (TREES, SPANS), 1, segment // 2 + 1)
    column = jnp.arange(SPANS, dtype=jnp.int32)
    starts = column[None, :] * segment + offsets
    ends = jnp.where(column[None, :] == SPANS - 1, TOKENS, starts + sizes)
    return jnp.stack([starts, ends], axis=-1).astype(jnp.int32)


def levels(key, dims, shards, low, largest):
    gain = 1.0
    for position, blocks in shards:
        draws = jax.random.uniform(jax.random.fold_in(jax.random.fold_in(key, 6), position), (blocks,), jnp.float32, low / len(shards), largest / len(shards))
        gain = gain * jnp.repeat(jnp.exp(draws), dims[position] // blocks).reshape((-1,) + (1,) * (len(dims) - 1 - position))
    return gain


def normal_values(stream_key, extent, spread, most, cuts=(), held_as=jnp.bfloat16):
    level = levels(stream_key, extent, cuts, -0.22, 0.18) if cuts else 1.0
    array = jax.random.normal(stream_key, extent, jnp.float32) * spread * level
    return jnp.minimum(jnp.maximum(array, -most), most).astype(held_as)


def setup_inputs(seed: int = 0) -> dict:
    arg_keys = jax.random.split(jax.random.key(seed), 11)
    return {
        "queries": draw_queries(jax.random.fold_in(arg_keys[10], 71), 0),
        "keys": draw_keys(jax.random.fold_in(arg_keys[10], 71), 0),
        "values": normal_values(arg_keys[2], (TREES, TOKENS, KVH * DH), 1.0, 6.0, ((0, 16), (1, 16))),
        "saved_output": normal_values(arg_keys[3], (TREES, TOKENS, QH * DH), 1.0, 6.0, ((0, 16), (1, 16))),
        "output_grad": normal_values(arg_keys[4], (TREES, TOKENS, QH * DH), 1.0, 6.0, ((0, 16), (1, 16))),
        "log_sums": draw_log_sums(jax.random.fold_in(arg_keys[10], 71), 0),
        "layer_input": normal_values(arg_keys[6], (TREES, TOKENS, D), 1.0, 6.0, ((0, 16), (1, 16))),
        "parents": draw_parents(jax.random.fold_in(arg_keys[10], 71), 0),
        "placement": draw_placement(jax.random.fold_in(arg_keys[10], 71), 0),
        "tool_spans": draw_tool_spans(jax.random.fold_in(arg_keys[10], 71), 0),
    }


HIGHEST = lax.Precision.HIGHEST

def visibility(parent_row, placement_row):
    count = parent_row.shape[0]
    steps = jax.nn.one_hot(parent_row, count, dtype=jnp.float32)
    identity = jnp.eye(count, dtype=jnp.float32)

    def climb(index, state):
        reach, walker = state
        walker = jnp.dot(walker, steps, precision=HIGHEST)
        return (jnp.maximum(reach, walker), walker)
    reach, walker = lax.fori_loop(0, count, climb, (identity, identity))
    placed = jax.nn.one_hot(placement_row, count, dtype=jnp.float32)
    return jnp.dot(jnp.dot(placed, reach, precision=HIGHEST), placed.T, precision=HIGHEST)

def tree_backward(operands):
    queries, keys, values, saved_output, output_grad, log_sums, layer_input, parent_row, placement_row, span_row = operands
    group_size = QH // KVH
    score_scale = 1.0 / math.sqrt(DH)
    visible = visibility(parent_row, placement_row)
    positions = jnp.arange(TOKENS, dtype=jnp.int32)
    slots = positions // BLOCK
    slot_hits = jax.nn.one_hot(slots, BLOCKS, dtype=jnp.float32)
    linked = jnp.dot(jnp.dot(slot_hits, visible, precision=HIGHEST), slot_hits.T, precision=HIGHEST) > 0.5
    allowed = linked & ((slots[:, None] != slots[None, :]) | (positions[None, :] <= positions[:, None]))
    inside = (positions[:, None] >= span_row[None, :, 0]) & (positions[:, None] < span_row[None, :, 1])
    scored = 1 - jnp.any(inside, axis=1).astype(jnp.int32)
    loss_grad = output_grad * scored.astype(jnp.bfloat16)[:, None]
    query_groups = queries.reshape(TOKENS, KVH, group_size, DH).transpose(1, 2, 0, 3)
    grad_groups = loss_grad.reshape(TOKENS, KVH, group_size, DH).transpose(1, 2, 0, 3)
    saved_groups = saved_output.reshape(TOKENS, KVH, group_size, DH).transpose(1, 2, 0, 3)
    log_groups = log_sums.reshape(KVH, group_size, TOKENS)
    key_groups = keys.reshape(TOKENS, KVH, DH).transpose(1, 0, 2)
    value_groups = values.reshape(TOKENS, KVH, DH).transpose(1, 0, 2)

    def one_group(pieces):
        query_part, grad_part, saved_part, log_part, key_part, value_part = pieces
        query_wide = query_part.astype(jnp.float32)
        grad_wide = grad_part.astype(jnp.float32)
        key_wide = key_part.astype(jnp.float32)
        value_wide = value_part.astype(jnp.float32)
        scores = jnp.einsum('hqd,kd->hqk', query_wide, key_wide, precision=HIGHEST) * score_scale
        probs = jnp.where(allowed[None], jnp.exp(scores - log_part[:, :, None]), 0.0)
        row_dots = lax.optimization_barrier(jnp.sum(grad_wide * saved_part.astype(jnp.float32), axis=-1))
        dprobs = jnp.einsum('hqd,kd->hqk', grad_wide, value_wide, precision=HIGHEST)
        slopes = (probs * (dprobs - row_dots[:, :, None]) * score_scale).astype(jnp.bfloat16)
        slopes = lax.optimization_barrier(slopes).astype(jnp.float32)
        probs_half = lax.optimization_barrier(probs.astype(jnp.bfloat16)).astype(jnp.float32)
        query_grad = jnp.einsum('hqk,kd->hqd', slopes, key_wide, precision=HIGHEST).astype(jnp.bfloat16)
        key_grad = jnp.einsum('hqk,hqd->kd', slopes, query_wide, precision=HIGHEST).astype(jnp.bfloat16)
        value_grad = jnp.einsum('hqk,hqd->kd', probs_half, grad_wide, precision=HIGHEST).astype(jnp.bfloat16)
        return (query_grad, key_grad, value_grad)
    query_grad, key_grad, value_grad = lax.map(one_group, (query_groups, grad_groups, saved_groups, log_groups, key_groups, value_groups))
    query_grad = query_grad.transpose(2, 0, 1, 3).reshape(TOKENS, QH * DH)
    key_grad = key_grad.transpose(1, 0, 2).reshape(TOKENS, KVH * DH)
    value_grad = value_grad.transpose(1, 0, 2).reshape(TOKENS, KVH * DH)
    weight_part = jnp.dot(value_grad.T, layer_input, preferred_element_type=jnp.float32)
    return (query_grad, key_grad, value_grad, weight_part)

def reference(queries, keys, values, saved_output, output_grad, log_sums, layer_input, parents, placement, tool_spans):
    query_grad, key_grad, value_grad, weight_parts = lax.map(tree_backward, (queries, keys, values, saved_output, output_grad, log_sums, layer_input, parents, placement, tool_spans))
    weight_grad = lax.optimization_barrier(jnp.sum(weight_parts, axis=0)) / TREES
    return (query_grad, key_grad, value_grad, weight_grad)
```

```python
import functools, math
import jax
import jax.numpy as jnp
from jax.sharding import PartitionSpec as P
from jax import lax
from jax.experimental import pallas as pl
from jax.experimental.pallas import tpu as pltpu
bf16=jnp.bfloat16; f32=jnp.float32; i32=jnp.int32
QH=48; KVH=4; DH=128; BLOCK=128; GS=QH//KVH; GW=GS*DH
SCALE=1.0/math.sqrt(DH); LOG2E=math.log2(math.e)

def dot(a,b):
    return jnp.dot(a,b,preferred_element_type=f32)

def vis_kernel(place_ref, parents_ref, placement_ref, out_ref, anc_ref):
    z=place_ref[0]; xl=place_ref[1]; nz=place_ref[2]
    def clear(i,c):
        anc_ref[i]=0
        out_ref[i]=0
        return c
    lax.fori_loop(0,16,clear,0)
    def climb(i,b):
        anc_ref[b]=1
        return parents_ref[b]
    lax.fori_loop(0,16,climb,placement_ref[z*2+xl])
    def put(r,n):
        u=lax.rem(z+r//2,nz)*2+(xl+r%2)%2
        hit=anc_ref[placement_ref[u]]
        @pl.when(hit==1)
        def _():
            out_ref[n]=r
        return n+hit
    out_ref[16]=lax.fori_loop(0,16,put,0)

def visible_list(place,parents,placement):
    sm=pl.BlockSpec(memory_space=pltpu.SMEM)
    return pl.pallas_call(vis_kernel,out_shape=jax.ShapeDtypeStruct((17,),i32),in_specs=[sm]*3,out_specs=sm,
        scratch_shapes=[pltpu.SMEM((16,),i32)],name="visible_list")(place,parents,placement)

def prep_kernel(base_ref, spans_ref, q_ref, do_ref, o_ref, l_ref, qt_ref, qs_ref, dot_ref, dos_ref, rd_ref, l2_ref):
    pos=base_ref[0]+lax.broadcasted_iota(i32,(BLOCK,DH),0)
    inside=jnp.zeros((BLOCK,DH),jnp.bool_)
    for m in range(8):
        inside=inside|((pos>=spans_ref[m,0])&(pos<spans_ref[m,1]))
    scored=jnp.where(inside,0.0,1.0)
    for h in range(GS):
        c=slice(h*DH,(h+1)*DH)
        q=q_ref[:,c]
        g=do_ref[:,c].astype(f32)*scored
        gb=g.astype(bf16)
        qt_ref[:,c]=q.T
        qs_ref[c,:]=q
        dot_ref[:,c]=gb.T
        dos_ref[c,:]=gb
        rd_ref[0,:,c]=jnp.sum((g*o_ref[:,c].astype(f32)).T,axis=0,keepdims=True)
        l2_ref[0,:,c]=l_ref[0,h:h+1,:]*LOG2E

def prep(base,spans,q,do,o,l):
    sm=pl.BlockSpec(memory_space=pltpu.SMEM)
    nat=pl.BlockSpec((BLOCK,GW),lambda g:(0,g))
    tr=pl.BlockSpec((DH,GW),lambda g:(g,0))
    st=pl.BlockSpec((GW,DH),lambda g:(g,0))
    row=pl.BlockSpec((1,1,GW),lambda g:(g,0,0))
    ng=KVH
    s=jax.ShapeDtypeStruct
    return pl.pallas_call(prep_kernel,grid=(ng,),
        in_specs=[sm,sm,nat,nat,nat,pl.BlockSpec((1,GS,BLOCK),lambda g:(g,0,0))],
        out_specs=[tr,st,tr,st,row,row],
        out_shape=[s((ng*DH,GW),bf16),s((ng*GW,DH),bf16),s((ng*DH,GW),bf16),s((ng*GW,DH),bf16),s((ng,1,GW),f32),s((ng,1,GW),f32)],
        compiler_params=pltpu.CompilerParams(vmem_limit_bytes=48<<20),name="prep")(base,spans,q,do,o,l.reshape(ng,GS,BLOCK))

CW=512
def diag_mask(width):
    k=lax.broadcasted_iota(i32,(BLOCK,width),0)
    q=lax.broadcasted_iota(i32,(BLOCK,width),1)%BLOCK
    return k<=q

def over_visible(vis_ref, single, pair):
    n=vis_ref[16]
    single(0,True)
    def body(i,c):
        pair(vis_ref[1+2*i],vis_ref[2+2*i])
        return c
    lax.fori_loop(0,(n-1)//2,body,0)
    @pl.when(lax.rem(n-1,2)==1)
    def _():
        single(vis_ref[n-1],False)

def rows_of(ref,blk):
    return ref[pl.ds(pl.multiple_of(blk*BLOCK,BLOCK),BLOCK),:]

def gather_in(parts, held):
    n=parts[0].shape[0]
    for i,p in enumerate(parts):
        held[i*n:(i+1)*n,:]=p[...]
def scatter_out(held, parts):
    n=parts[0].shape[0]
    for i,p in enumerate(parts):
        p[...]=held[i*n:(i+1)*n,:]

def value_kernel(np_, vis_ref, qt_ref, dos_ref, l2_ref, *refs):
    ks=refs[:np_]; outs=refs[np_:2*np_]; k_all, dv_all, p_buf = refs[2*np_:]
    gather_in(ks,k_all)
    dv_all[...]=jnp.zeros_like(dv_all)
    def probs(k,rows,masked):
        for c in range(0,GW,CW):
            s=dot(k,qt_ref[:,c:c+CW])
            p=jnp.exp2(s*(SCALE*LOG2E)-l2_ref[0,:,c:c+CW])
            if masked: p=jnp.where(diag_mask(CW),p,0.0)
            p_buf[:rows,c:c+CW]=p.astype(bf16)
        return dot(p_buf[:rows,:],dos_ref[...]).astype(bf16)
    def put(ref,blk,v):
        ref[pl.ds(pl.multiple_of(blk*BLOCK,BLOCK),BLOCK),:]=v
    def single(b,masked):
        put(dv_all,b,probs(rows_of(k_all,b),BLOCK,masked))
    def pair(a,b):
        v=probs(jnp.concatenate([rows_of(k_all,a),rows_of(k_all,b)],0),2*BLOCK,False)
        put(dv_all,a,v[:BLOCK]); put(dv_all,b,v[BLOCK:])
    over_visible(vis_ref,single,pair)
    scatter_out(dv_all,outs)

def value_pass(vis,qt,dos,l2,ks,groups):
    np_=len(ks); rows=ks[0].shape[0]; tot=np_*rows
    g0,g1=groups; ng=g1-g0
    s=jax.ShapeDtypeStruct
    gs=pltpu.PrefetchScalarGridSpec(num_scalar_prefetch=1,grid=(ng,),
        in_specs=[pl.BlockSpec((DH,GW),lambda g,v:(g+g0,0)),pl.BlockSpec((GW,DH),lambda g,v:(g+g0,0)),pl.BlockSpec((1,1,GW),lambda g,v:(g+g0,0,0))]
            +[pl.BlockSpec((rows,DH),lambda g,v:(0,g+g0))]*np_,
        out_specs=[pl.BlockSpec((rows,DH),lambda g,v:(0,g))]*np_,
        scratch_shapes=[pltpu.VMEM((tot,DH),bf16),pltpu.VMEM((tot,DH),bf16),pltpu.VMEM((2*BLOCK,GW),bf16)])
    return pl.pallas_call(functools.partial(value_kernel,np_),grid_spec=gs,out_shape=[s((rows,ng*DH),bf16)]*np_,
        compiler_params=pltpu.CompilerParams(vmem_limit_bytes=48<<20),
        cost_estimate=pl.CostEstimate(flops=ng*2*2*tot*GW*DH,bytes_accessed=ng*4*tot*DH,transcendentals=ng*tot*GW),
        name="value_pass")(vis,qt,dos,l2,*ks)

def key_kernel(np_, vis_ref, qt_ref, qs_ref, dot_ref, l2_ref, rd_ref, *refs):
    ks=refs[:np_]; vs=refs[np_:2*np_]; dq_ref=refs[2*np_]; outs=refs[2*np_+1:3*np_+1]; k_all, v_all, dk_all, s_buf, dqt = refs[3*np_+1:]
    gather_in(ks,k_all); gather_in(vs,v_all)
    dk_all[...]=jnp.zeros_like(dk_all)
    dqt[...]=jnp.zeros_like(dqt)
    def slopes(k,v,rows,masked):
        kt=k.T
        for c in range(0,GW,CW):
            s=dot(k,qt_ref[:,c:c+CW])
            p=jnp.exp2(s*(SCALE*LOG2E)-l2_ref[0,:,c:c+CW])
            if masked: p=jnp.where(diag_mask(CW),p,0.0)
            d=dot(v,dot_ref[:,c:c+CW])
            sl=(p*(d-rd_ref[0,:,c:c+CW])*SCALE).astype(bf16)
            s_buf[:rows,c:c+CW]=sl
            dqt[:,c:c+CW]+=dot(kt,sl)
        return dot(s_buf[:rows,:],qs_ref[...]).astype(bf16)
    def put(ref,blk,v):
        ref[pl.ds(pl.multiple_of(blk*BLOCK,BLOCK),BLOCK),:]=v
    def single(b,masked):
        put(dk_all,b,slopes(rows_of(k_all,b),rows_of(v_all,b),BLOCK,masked))
    def pair(a,b):
        v=slopes(jnp.concatenate([rows_of(k_all,a),rows_of(k_all,b)],0),jnp.concatenate([rows_of(v_all,a),rows_of(v_all,b)],0),2*BLOCK,False)
        put(dk_all,a,v[:BLOCK]); put(dk_all,b,v[BLOCK:])
    over_visible(vis_ref,single,pair)
    scatter_out(dk_all,outs)
    for h in range(GS):
        c=slice(h*DH,(h+1)*DH)
        dq_ref[:,c]=dqt[:,c].T.astype(bf16)

def key_pass(vis,qt,qs,dot_,l2,rd,ks,vs,groups):
    np_=len(ks); rows=ks[0].shape[0]; tot=np_*rows
    g0,g1=groups; ng=g1-g0
    s=jax.ShapeDtypeStruct
    tr=pl.BlockSpec((DH,GW),lambda g,v:(g+g0,0)); st=pl.BlockSpec((GW,DH),lambda g,v:(g+g0,0)); row=pl.BlockSpec((1,1,GW),lambda g,v:(g+g0,0,0))
    gs=pltpu.PrefetchScalarGridSpec(num_scalar_prefetch=1,grid=(ng,),
        in_specs=[tr,st,tr,row,row]+[pl.BlockSpec((rows,DH),lambda g,v:(0,g+g0))]*(2*np_),
        out_specs=[pl.BlockSpec((BLOCK,GW),lambda g,v:(0,g))]+[pl.BlockSpec((rows,DH),lambda g,v:(0,g))]*np_,
        scratch_shapes=[pltpu.VMEM((tot,DH),bf16)]*3+[pltpu.VMEM((2*BLOCK,GW),bf16),pltpu.VMEM((DH,GW),f32)])
    r=pl.pallas_call(functools.partial(key_kernel,np_),grid_spec=gs,out_shape=[s((BLOCK,ng*GW),bf16)]+[s((rows,ng*DH),bf16)]*np_,
        compiler_params=pltpu.CompilerParams(vmem_limit_bytes=48<<20),
        cost_estimate=pl.CostEstimate(flops=ng*4*2*tot*GW*DH,bytes_accessed=ng*6*tot*DH,transcendentals=ng*tot*GW),
        name="key_pass")(vis,qt,qs,dot_,l2,rd,*ks,*vs)
    return r[0],r[1:]


def weight_kernel(np_, place_ref, x_ref, *refs):
    vgs = refs[:np_]
    out_ref, vg_t, x_all = refs[np_:]
    z, xl, nz = place_ref[0], place_ref[1], place_ref[2]
    for i, part in enumerate(vgs):
        for j in range(2):
            rows = slice(j * BLOCK, (j + 1) * BLOCK)
            at = slice((2 * i + j) * BLOCK, (2 * i + j + 1) * BLOCK)
            vg_t[:, at] = part[rows, :].T
            x_all[at, :] = x_ref[lax.rem(z + i, nz) * 2 + (xl + j) % 2]
    out_ref[...] = dot(vg_t[...], x_all[...]) * (1.0 / 16.0)


def weight_part(place, x, vgs):
    np_ = len(vgs)
    tot = np_ * 2 * BLOCK
    cols = x.shape[2]
    rows = vgs[0].shape[1]
    vm = pl.BlockSpec(memory_space=pltpu.VMEM)
    return pl.pallas_call(
        functools.partial(weight_kernel, np_),
        in_specs=[pl.BlockSpec(memory_space=pltpu.SMEM)] + [vm] * (np_ + 1),
        out_specs=vm,
        out_shape=jax.ShapeDtypeStruct((rows, cols), f32),
        scratch_shapes=[pltpu.VMEM((rows, tot), bf16), pltpu.VMEM((tot, cols), bf16)],
        compiler_params=pltpu.CompilerParams(vmem_limit_bytes=48 << 20),
        name="weight_part",
    )(place, x, *vgs)


def send(value, dz, dx):
    count = lax.axis_size("ctx")
    nz = count // 2
    pairs = [(z * 2 + x, (z + dz) % nz * 2 + (x ^ dx)) for z in range(nz) for x in range(2)]
    return lax.ppermute(value, "ctx", pairs)


def gather_ring(own):
    half = own.shape[0]
    nz = lax.axis_size("ctx") // 2
    mid = nz // 2
    pair = jnp.concatenate([own, send(own, 0, 1)], 0)
    parts = [pair] + [None] * (nz - 1)
    up = down = pair
    for k in range(1, mid):
        up, down = send(up, 1, 0), send(down, -1, 0)
        parts[nz - k], parts[k] = up, down
    parts[mid] = jnp.concatenate([send(up[:half], 1, 0), send(down[half:], -1, 0)], 0)
    return parts


def reduce_ring(parts):
    nz = len(parts)
    mid = nz // 2
    half = parts[0].shape[0] // 2
    wide = lambda v: v.astype(f32)
    up, down = send(parts[mid][:half], 1, 0), send(parts[mid][half:], -1, 0)
    for k in range(mid - 1, 0, -1):
        a, b = parts[k], parts[nz - k]
        if k == mid - 1:
            u = jnp.concatenate([(wide(a[:half]) + wide(up)).astype(bf16), a[half:]], 0)
            d = jnp.concatenate([b[:half], (wide(b[half:]) + wide(down)).astype(bf16)], 0)
        else:
            u = (wide(a) + wide(up)).astype(bf16)
            d = (wide(b) + wide(down)).astype(bf16)
        up, down = send(u, 1, 0), send(d, -1, 0)
    total = wide(parts[0]) + wide(up) + wide(down)
    return (total[:half] + wide(send(total[half:].astype(bf16), 0, 1))).astype(bf16)


def local(
    queries, keys, values, saved_output, output_grad, log_sums, layer_input, parents, placement, tool_spans
):
    ctx = lax.axis_index("ctx")
    nctx = lax.axis_size("ctx")
    ndp = lax.axis_size("dp")
    place = jnp.stack([ctx // 2, ctx % 2, jnp.int32(nctx // 2)]).astype(i32)
    base = (ctx * BLOCK).astype(i32)[None]
    k_parts = gather_ring(keys[0])
    v_parts = gather_ring(values[0])
    vis = visible_list(place, parents[0], placement[0])
    qt, qs, dot_, dos, rd, l2 = prep(base, tool_spans[0], queries[0], output_grad[0], saved_output[0], log_sums[0])
    cols = layer_input.shape[2] // nctx
    x = jnp.transpose(layer_input[0].reshape(BLOCK, nctx, cols), (1, 0, 2))
    x = lax.all_to_all(x, "ctx", 0, 0, tiled=True)
    dv_parts = value_pass(vis, qt, dos, l2, k_parts, (0, KVH))
    dq, dk = [], []
    for g in range(KVH):
        a, b = key_pass(vis, qt, qs, dot_, l2, rd, k_parts, v_parts, (g, g + 1))
        dq.append(a)
        dk.append(b)
    value_grad = reduce_ring(dv_parts)
    key_grad = reduce_ring([jnp.concatenate([d[r] for d in dk], 1) for r in range(len(dv_parts))])
    query_grad = jnp.concatenate(dq, 1)
    w = weight_part(place, x, gather_ring(value_grad))
    rows = w.shape[0] // ndp
    w = lax.all_to_all(w.reshape(ndp, rows, cols), "dp", 0, 0, tiled=True)
    w = jnp.sum(w, 0)
    w = lax.all_to_all(w.reshape(nctx, rows // nctx, cols), "ctx", 0, 0, tiled=True)
    weight_grad = jnp.transpose(w, (1, 0, 2)).reshape(rows // nctx, nctx * cols)
    return (query_grad[None], key_grad[None], value_grad[None], weight_grad)


def solution(mesh):
    return jax.shard_map(
        local,
        mesh=mesh,
        in_specs=(
            P("dp", "ctx", None),
            P("dp", "ctx", None),
            P("dp", "ctx", None),
            P("dp", "ctx", None),
            P("dp", "ctx", None),
            P("dp", None, "ctx"),
            P("dp", "ctx", None),
            P("dp", None),
            P("dp", None),
            P("dp", None, None),
        ),
        out_specs=(
            P("dp", "ctx", None),
            P("dp", "ctx", None),
            P("dp", "ctx", None),
            P(("dp", "ctx"), None),
        ),
        check_vma=False,
    )
```

```python
import functools
import math

import jax
import jax.numpy as jnp
from jax import lax
from jax.experimental import pallas as pl
from jax.experimental.pallas import tpu as pltpu
from jax.sharding import PartitionSpec as P

bf16 = jnp.bfloat16
f32 = jnp.float32
i32 = jnp.int32
QH, KVH, DH, BLOCK = 48, 4, 128, 128
GS = QH // KVH
GW = GS * DH
NZ = 8
TOK = 2 * NZ * BLOCK
MANY = 4
SCALE = 1.0 / math.sqrt(DH)
LOG2E = math.log2(math.e)
SMEM = pl.BlockSpec(memory_space=pltpu.SMEM)
VMEM = pl.BlockSpec(memory_space=pltpu.VMEM)
PARAMS = pltpu.CompilerParams(vmem_limit_bytes=60 << 20)
SIZES = (256, 256, 256, 256, 128, 128, 256, 256, 256)


def dot(a, b):
    return jnp.dot(a, b, preferred_element_type=f32)


def move(value, to):
    pairs = []
    for xh in range(2):
        for y in range(4):
            for c in range(2):
                for z in range(NZ):
                    for xl in range(2):
                        h2, y2, c2, z2, x2 = to(xh, y, c, z, xl)
                        flat = lambda a, b, d, e, f: ((a * 4 + b) * 2 + d) * 16 + e * 2 + f
                        pairs.append((flat(xh, y, c, z, xl), flat(h2, y2, c2, z2, x2)))
    return lax.ppermute(value, ("dp", "ctx"), [p for p in pairs if p[0] != p[1]])


def along_z(value, steps):
    return move(value, lambda h, y, c, z, x: (h, y, c, (z + steps) % NZ, x))


def moved0(value):
    return move(value, lambda h, y, c, z, x: (h, y, x, z, c))


def out0(value):
    stays = lax.axis_index("dp") % 2 == lax.axis_index("ctx") % 2
    return jnp.where(stays, value, moved0(value))


def out1(value):
    return move(value, lambda h, y, c, z, x: (h, y, 1 - x, z, c))


def back0(value):
    return out0(value)


def back1(value):
    return move(value, lambda h, y, c, z, x: (h, y, x, z, 1 - c))


def vis_kernel(place_ref, tree_ref, out_ref, anc_ref):
    z, core = place_ref[0], place_ref[2]
    for s in range(2):

        def clear(i, c):
            anc_ref[i] = 0
            out_ref[s, i] = 0
            return c

        lax.fori_loop(0, 16, clear, 0)

        def climb(i, b):
            anc_ref[b] = 1
            return tree_ref[0, b]

        lax.fori_loop(0, 16, climb, tree_ref[1, z * 2 + (core + s) % 2])
        out_ref[s, 0] = s

        def put(r, n):
            u = lax.rem(z + r // 2, NZ) * 2 + (core + r) % 2
            hit = jnp.where(r == s, 0, anc_ref[tree_ref[1, u]])

            @pl.when(hit == 1)
            def _():
                out_ref[s, n] = r

            return n + hit

        out_ref[s, 16] = lax.fori_loop(0, 16, put, 1)


def visible_lists(place, tree):
    return pl.pallas_call(
        vis_kernel,
        out_shape=jax.ShapeDtypeStruct((2, 17), i32),
        in_specs=[SMEM] * 2,
        out_specs=SMEM,
        scratch_shapes=[pltpu.SMEM((16,), i32)],
        name="visible_lists",
    )(place, tree)


def pieces(v):
    a = v.astype(bf16)
    v = v - a.astype(f32)
    b = v.astype(bf16)
    return a, b, (v - b.astype(f32)).astype(bf16)


def prep_kernel(turn, place_ref, q_ref, do_ref, o_ref, l_ref, *refs):
    out_ref = refs[-1]
    if turn == 0:
        x_ref, xs_ref, out_ref = refs
        n = xs_ref.shape[2]
        for k in range(4):
            xs_ref[k] = x_ref[:, k * n : (k + 1) * n]
    first = (((place_ref[1] + turn) % 2) * 2 + pl.program_id(0)) * GS
    pos = place_ref[3] + lax.broadcasted_iota(i32, (BLOCK, DH), 0)
    inside = jnp.zeros((BLOCK, DH), jnp.bool_)
    for m in range(8):
        inside = inside | ((pos >= place_ref[5 + 2 * m]) & (pos < place_ref[6 + 2 * m]))
    scored = jnp.where(inside, 0.0, 1.0)
    out_ref[:BLOCK, :GW] = q_ref[...]
    zero = jnp.zeros((16 - 6, DH), bf16)
    for h in range(GS):
        c = slice(h * DH, (h + 1) * DH)
        g = do_ref[:, c].astype(f32) * scored
        out_ref[:BLOCK, GW + h * DH : GW + (h + 1) * DH] = g.astype(bf16)
        logs = pieces(l_ref[pl.ds(first + h, 1), :] * LOG2E)
        dots = pieces(jnp.sum((g * o_ref[:, c].astype(f32)).T, axis=0, keepdims=True))
        out_ref[BLOCK:, c] = jnp.concatenate([*logs, *dots, zero], 0)
        out_ref[BLOCK:, GW + h * DH : GW + (h + 1) * DH] = jnp.zeros((16, DH), bf16)


def prep(place, q, do, o, logs, turn, x=None):
    half = lambda i, p: ((p[1] + turn) % 2) * 2 + i
    nat = pl.BlockSpec((BLOCK, GW), lambda i, p: (0, half(i, p)))
    ins, args = [nat, nat, nat, pl.BlockSpec((QH, BLOCK), lambda i, p: (0, 0))], [q, do, o, logs]
    outs = [pl.BlockSpec((BLOCK + 16, 2 * GW), lambda i, p: (0, i))]
    shapes = [jax.ShapeDtypeStruct((BLOCK + 16, 4 * GW), bf16)]
    if x is not None:
        n = x.shape[1] // 8
        ins, args = ins + [pl.BlockSpec((BLOCK, 4 * n), lambda i, p: (0, i))], args + [x]
        outs = [pl.BlockSpec((4, BLOCK, n), lambda i, p: (i, 0, 0))] + outs
        shapes = [jax.ShapeDtypeStruct((8, BLOCK, n), bf16)] + shapes
    return pl.pallas_call(
        functools.partial(prep_kernel, turn),
        grid_spec=pltpu.PrefetchScalarGridSpec(num_scalar_prefetch=1, grid=(2,), in_specs=ins, out_specs=outs),
        out_shape=shapes,
        compiler_params=PARAMS,
        cost_estimate=pl.CostEstimate(flops=10**6, bytes_accessed=3 * 10**6, transcendentals=0),
        name="prep",
    )(place, *args)


def row_of(q_ref, at):
    p = q_ref[BLOCK:, :].astype(f32)
    return p[at : at + 1] + p[at + 1 : at + 2] + p[at + 2 : at + 3]


def over_visible(vis_ref, s, part):
    n = vis_ref[s, 16] - 1
    part([s], True)

    def body(i, c):
        part([vis_ref[s, 1 + MANY * i + k] for k in range(MANY)], False)
        return c

    lax.fori_loop(0, n // MANY, body, 0)
    left = MANY // 2
    while left:
        at = 1 + n // (2 * left) * (2 * left)

        @pl.when(n // left % 2 == 1)
        def _():
            part([vis_ref[s, at + k] for k in range(left)], False)

        left //= 2


def rows(blk):
    return pl.ds(pl.multiple_of(blk * BLOCK, BLOCK), BLOCK)


def taken(ref, blocks):
    return jnp.concatenate([ref[rows(b), :] for b in blocks], 0)


def added(ref, blocks, v):
    for i, b in enumerate(blocks):
        ref[rows(b), :] += v[i * BLOCK : (i + 1) * BLOCK]


def fill(held, parts):
    at = 0
    for p in parts:
        n = p.shape[0]
        held[at : at + n, :] = p[...]
        at += n


def spill(held, parts):
    at = 0
    for p in parts:
        n = p.shape[0]
        p[:, -DH:] = held[at : at + n, :].astype(bf16)
        at += n


def masked_if(diag, p):
    if not diag:
        return p
    k = lax.broadcasted_iota(i32, p.shape, 0)
    q = lax.broadcasted_iota(i32, p.shape, 1) % BLOCK
    return jnp.where(k <= q, p, 0.0)


def setup_kernel(turn, place_ref, *refs):
    t_ref, n_ref, r_ref = refs[-3:]
    q, g = refs[0][...], refs[1][...]
    if turn == 0:
        stays = place_ref[1] == place_ref[2]
        q, g = jnp.where(stays, refs[2][...], q), jnp.where(stays, refs[3][...], g)
    for i, v in enumerate((q, g)):
        for h in range(GS):
            c = slice(h * DH, (h + 1) * DH)
            t_ref[0, i * DH : (i + 1) * DH, c] = v[:BLOCK, c].T
            n_ref[0, i * GW + h * DH : i * GW + (h + 1) * DH, :] = v[:BLOCK, c]
    r_ref[0, 0:1, :] = row_of(q, 0)
    r_ref[0, 1:2, :] = row_of(q, 3)


def setup(place, turn, *given):
    nat = [pl.BlockSpec((BLOCK + 16, GW), lambda i, p, k=k: (0, 2 * i + k)) for k in range(2)]
    shapes = [((2 * DH, GW), bf16), ((2 * GW, DH), bf16), ((2, GW), f32)]
    return pl.pallas_call(
        functools.partial(setup_kernel, turn),
        grid_spec=pltpu.PrefetchScalarGridSpec(
            num_scalar_prefetch=1,
            grid=(2,),
            in_specs=nat * len(given),
            out_specs=[pl.BlockSpec((1, *n), lambda i, p: (i, 0, 0)) for n, _ in shapes],
        ),
        out_shape=[jax.ShapeDtypeStruct((2, *n), t) for n, t in shapes],
        compiler_params=PARAMS,
        cost_estimate=pl.CostEstimate(flops=10**6, bytes_accessed=5 * 10**6, transcendentals=0),
        name="setup",
    )(place, *[v for v in given for _ in range(2)])


def value_kernel(vis_ref, *refs):
    np_ = len(SIZES)
    slots, refs = (refs[:3], refs[3:6]), refs[6:]
    ks, outs = refs[:np_], refs[np_ : 2 * np_]
    k_all, dv_all, p_buf = refs[2 * np_ :]
    fill(k_all, ks)
    dv_all[...] = jnp.zeros_like(dv_all)
    for s, (t_ref, n_ref, r_ref) in enumerate(slots):

        def part(blocks, diag, t_ref=t_ref, n_ref=n_ref, r_ref=r_ref):
            k, n = taken(k_all, blocks), len(blocks) * BLOCK
            p = jnp.exp2(dot(k, t_ref[0]) * (SCALE * LOG2E) - r_ref[0, 0:1, :])
            p_buf[:n, :] = masked_if(diag, p).astype(bf16)
            added(dv_all, blocks, dot(p_buf[:n, :], n_ref[0]))

        over_visible(vis_ref, s, part)
    spill(dv_all, outs)


def value_pass(vis, ready, kvs):
    part = [pl.BlockSpec((n, DH), lambda i, v: (0, i)) for n in SIZES]
    return pl.pallas_call(
        value_kernel,
        grid_spec=pltpu.PrefetchScalarGridSpec(
            num_scalar_prefetch=1,
            grid=(2,),
            in_specs=[
                pl.BlockSpec((1, DH, GW), lambda i, v: (i, 0, 0)),
                pl.BlockSpec((1, GW, DH), lambda i, v: (i, 1, 0)),
                pl.BlockSpec((1, 2, GW), lambda i, v: (i, 0, 0)),
            ]
            * 2
            + part,
            out_specs=part,
            scratch_shapes=[
                pltpu.VMEM((TOK, DH), bf16),
                pltpu.VMEM((TOK, DH), f32),
                pltpu.VMEM((MANY * BLOCK, GW), bf16),
            ],
        ),
        out_shape=[jax.ShapeDtypeStruct((n, 2 * DH), bf16) for n in SIZES],
        compiler_params=PARAMS,
        cost_estimate=pl.CostEstimate(flops=8 * 10**9, bytes_accessed=8 * 10**6, transcendentals=6 * 10**6),
        name="value_pass",
    )(vis, *ready, *kvs)


def key_kernel(vis_ref, *refs):
    np_ = len(SIZES)
    slots, refs = (refs[:3], refs[3:6]), refs[6:]
    ks, vs, refs = refs[:np_], refs[np_ : 2 * np_], refs[2 * np_ :]
    others = refs[: -np_ - 7]
    dqs, outs = refs[-np_ - 7 : -np_ - 5], refs[-np_ - 5 : -5]
    k_all, v_all, dk_all, s_buf, dqt = refs[-5:]
    fill(k_all, ks)
    fill(v_all, vs)
    dk_all[...] = jnp.zeros_like(dk_all)
    for s, (t_ref, n_ref, r_ref) in enumerate(slots):
        dqt[...] = jnp.zeros_like(dqt)

        def part(blocks, diag, t_ref=t_ref, n_ref=n_ref, r_ref=r_ref):
            k, v, n = taken(k_all, blocks), taken(v_all, blocks), len(blocks) * BLOCK
            logs = r_ref[0, 0:1, :] - math.log2(SCALE)
            p = jnp.exp2(dot(k, t_ref[0, :DH, :]) * (SCALE * LOG2E) - logs)
            d = dot(v, t_ref[0, DH:, :]) - r_ref[0, 1:2, :]
            s_buf[:n, :] = (masked_if(diag, p) * d).astype(bf16)
            dqt[...] += dot(k.T, s_buf[:n, :])
            added(dk_all, blocks, dot(s_buf[:n, :], n_ref[0]))

        over_visible(vis_ref, s, part)
        for h in range(GS):
            c = slice(h * DH, (h + 1) * DH)
            dqs[s][:, c] = dqt[:, c].T.astype(bf16)
    spill(dk_all, outs)
    for o, p in zip(outs, others):
        o[:, :DH] = p[...]


def key_pass(vis, group, ready, kvs, others=()):
    part = [pl.BlockSpec((n, DH), lambda i, v, k=k: (0, group + 2 * k)) for k in range(2) for n in SIZES]
    whole = lambda shape: pl.BlockSpec(shape, lambda i, v: (0, 0))
    dq = [jax.ShapeDtypeStruct((BLOCK, GW), bf16)] * 2
    dk = [jax.ShapeDtypeStruct((n, (group + 1) * DH), bf16) for n in SIZES]
    out = pl.pallas_call(
        key_kernel,
        grid_spec=pltpu.PrefetchScalarGridSpec(
            num_scalar_prefetch=1,
            grid=(1,),
            in_specs=[
                pl.BlockSpec((1, 2 * DH, GW), lambda i, v: (group, 0, 0)),
                pl.BlockSpec((1, GW, DH), lambda i, v: (group, 0, 0)),
                pl.BlockSpec((1, 2, GW), lambda i, v: (group, 0, 0)),
            ]
            * 2
            + part
            + [whole(m.shape) for m in others],
            out_specs=[whole(d.shape) for d in dq + dk],
            scratch_shapes=[
                pltpu.VMEM((TOK, DH), bf16),
                pltpu.VMEM((TOK, DH), bf16),
                pltpu.VMEM((TOK, DH), f32),
                pltpu.VMEM((MANY * BLOCK, GW), bf16),
                pltpu.VMEM((DH, GW), f32),
            ],
        ),
        out_shape=dq + dk,
        compiler_params=PARAMS,
        cost_estimate=pl.CostEstimate(flops=8 * 10**9, bytes_accessed=8 * 10**6, transcendentals=4 * 10**6),
        name="key_pass",
    )(vis, *ready, *kvs, *kvs, *others)
    return out[:2], out[2:]


def weight_kernel(place_ref, x_ref, *refs):
    np_ = len(refs) - 5
    vgs = refs[:np_]
    keep_ref, give_ref, vg_all, vg_t, x_all = refs[np_:]
    core, y = place_ref[2], place_ref[4]
    fill(vg_all, vgs)
    for i in range(8):
        at = slice(i * BLOCK, (i + 1) * BLOCK)
        x_all[at, :] = x_ref[lax.rem(y + i // 2, 4) * 2 + (core + i) % 2]
        vg_t[:, at] = vg_all[at, :].T
    n = vg_t.shape[0]
    i = lax.broadcasted_iota(i32, (n, n), 0)
    bits = lambda k, m: lax.shift_right_logical(i, k) & m
    row = bits(7, 1) * 256 + bits(1, 7) * 32 + bits(4, 7) * 4 + (bits(8, 1) ^ place_ref[1]) * 2 + bits(0, 1)
    order = jnp.where(row == lax.broadcasted_iota(i32, (n, n), 1), 1.0, 0.0).astype(bf16)
    turned_rows = dot(order, vg_t[...]).astype(bf16)
    w = dot(turned_rows, x_all[...]) * (1.0 / 16.0)
    keep_ref[...] = w[: n // 2]
    give_ref[...] = w[n // 2 :].astype(bf16)


def weight_part(place, x, vgs):
    tot = 8 * BLOCK
    n, cols = vgs[0].shape[1], x.shape[2]
    return pl.pallas_call(
        weight_kernel,
        in_specs=[SMEM] + [VMEM] * (len(vgs) + 1),
        out_specs=[VMEM] * 2,
        out_shape=[jax.ShapeDtypeStruct((n // 2, cols), t) for t in (f32, bf16)],
        scratch_shapes=[pltpu.VMEM((tot, n), bf16), pltpu.VMEM((n, tot), bf16), pltpu.VMEM((tot, cols), bf16)],
        compiler_params=PARAMS,
        cost_estimate=pl.CostEstimate(flops=10**9, bytes_accessed=4 * 10**6, transcendentals=0),
        name="weight_part",
    )(place, x, *vgs)


def along_y(value, steps):
    return move(value, lambda h, y, c, z, x: (h, (y + steps) % 4, c, z, x))


def other_core(value):
    return move(value, lambda h, y, c, z, x: (h, y, 1 - c, z, x))


def other_x(value):
    return move(value, lambda h, y, c, z, x: (h, y, c, z, 1 - x))


def dealt(value, members):
    return lax.all_to_all(value, ("dp", "ctx"), 0, 0, axis_index_groups=members, tiled=True)


def device(xh, y, c, z, xl):
    return ((xh * 4 + y) * 2 + c) * 16 + z * 2 + xl


OVER_Y = [
    [device(h, y, c, z, x) for y in range(4) for c in range(2)] for h in range(2) for z in range(NZ) for x in range(2)
]
OVER_Z = [
    [device(h, y, c, z, x) for h in range(2) for z in range(NZ)] for y in range(4) for c in range(2) for x in range(2)
]


def near(own):
    return along_z(own, 2), along_z(own, -2), along_z(own, 1), along_z(own, -1)


def far(own, got):
    a2, b2, a1, b1 = got
    h = own.shape[0] // 2
    a3, b3 = along_z(a2, 1), along_z(b2, -1)
    a4, b4 = along_z(a2[:h], 2), along_z(b2[h:], -2)
    return [own, b1, b2, b3, a4, b4, a3, a2, a1]


def wide(v):
    return v.astype(f32)


def reduce_far(parts):
    p0, p1, p2, p3, p4a, p4b, p5, p6, p7 = parts
    return along_z(p3, 1), along_z(p5, -1), along_z(p4a, 2), along_z(p4b, -2), along_z(p1, 1), along_z(p7, -1)


def reduce_near(parts, got):
    p2, p6 = parts[2], parts[7]
    a, b, c, d = got[:4]
    h = c.shape[0]
    zero = jnp.zeros_like(c, f32)
    u = wide(p2) + wide(a) + jnp.concatenate([wide(c), zero], 0)
    v = wide(p6) + wide(b) + jnp.concatenate([zero, wide(d)], 0)
    return along_z(u.astype(bf16), 2), along_z(v.astype(bf16), -2)


def reduce_end(parts, got, last):
    total = wide(parts[0]) + wide(got[4]) + wide(got[5]) + wide(last[0]) + wide(last[1])
    return total.astype(bf16)


def home(value, xl):
    h = value.shape[0] // 2
    a, b = back0(value[:h]), back1(value[h:])
    return jnp.where(xl == 0, jnp.concatenate([a, b], 1), jnp.concatenate([b, a], 1))


def tie(*values):
    return lax.optimization_barrier(values)


def local(
    queries, keys, values, saved_output, output_grad, log_sums, layer_input, parents, placement, tool_spans
):
    ctx, dp = lax.axis_index("ctx"), lax.axis_index("dp")
    z, xl = ctx // 2, ctx % 2
    core, y = dp % 2, dp // 2 % 4
    place = jnp.concatenate([jnp.stack([z, xl, core, ctx * BLOCK, y]).astype(i32), tool_spans[0].reshape(16)])
    half = lambda v, t: lax.dynamic_slice_in_dim(v, ((xl + t) % 2) * 2 * DH, 2 * DH, 1)
    kv = [jnp.concatenate([half(keys[0], t), half(values[0], t)], 1) for t in range(2)]
    tree = jnp.concatenate([parents, placement], 0)
    place, kv, tree = tie(place, kv, tree)
    tree = out0(tree)
    kv = jnp.concatenate([out0(kv[0]), out1(kv[1])], 0)
    arrays = (queries[0], output_grad[0], saved_output[0], log_sums[0])
    (qg1,) = prep(place, *arrays, 1)
    x, qg0 = prep(place, *arrays, 0, layer_input[0])
    qg0, qg1, kv, tree, x = tie(qg0, qg1, kv, tree, x)
    kv_near = near(kv)
    moved1 = out1(qg1)
    vis = visible_lists(place, tree)
    kv_near, qg0, x, vis = tie(kv_near, qg0, x, vis)
    kvs = far(kv, kv_near)
    early = moved0(qg0)
    x = dealt(x, OVER_Y)
    ready = (*setup(place, 0, early, qg0), *setup(place, 1, moved1))
    kvs, ready, vis, x = tie(kvs, ready, vis, x)

    dvs = value_pass(vis, ready, kvs)
    got = reduce_far(dvs)
    ready, dvs = tie(ready, dvs)
    dq0, dk0 = key_pass(vis, 0, ready, kvs)
    got, dk0, dq0 = tie(got, dk0, dq0)
    last = reduce_near(dvs, got)
    dq0 = [back0(dq0[0]), back1(dq0[1])]
    dq1, dks = key_pass(vis, 1, ready, kvs, dk0)
    last, dks, dq1 = tie(last, dks, dq1)
    value_grad = home(reduce_end(dvs, got, last), xl)
    value_grad, dks, dq1 = tie(value_grad, dks, dq1)
    dk_got = reduce_far(dks)
    pair = jnp.concatenate([value_grad, other_core(value_grad)], 0)
    pair, dq1 = tie(pair, dq1)
    y1, y3 = along_y(pair, -1), along_y(pair, 1)
    dq1 = [back0(dq1[0]), back1(dq1[1])]
    vgs = [pair, y1, along_y(y3[:BLOCK], 1), along_y(y1[BLOCK:], -1), y3]
    vgs, dk_got = tie(vgs, dk_got)
    dk_last = reduce_near(dks, dk_got)
    keep, give = weight_part(place, x, vgs)
    w = keep + wide(other_x(give))
    w, dk_last = tie(w, dk_last)
    cols = w.shape[1]
    w = dealt(w.reshape(16, 16, cols), OVER_Z)
    key_grad = home(reduce_end(dks, dk_got, dk_last), xl)
    w = dealt(jnp.sum(w, 0).reshape(8, 2, cols), OVER_Y)
    weight_grad = jnp.transpose(w, (1, 0, 2)).reshape(2, 8 * cols)
    query_grad = jnp.where(
        xl == 0,
        jnp.concatenate([dq0[0], dq1[0], dq0[1], dq1[1]], 1),
        jnp.concatenate([dq0[1], dq1[1], dq0[0], dq1[0]], 1),
    )
    return (query_grad[None], key_grad[None], value_grad[None], weight_grad)


def solution(mesh):
    return jax.shard_map(
        local,
        mesh=mesh,
        in_specs=(
            P("dp", "ctx", None),
            P("dp", "ctx", None),
            P("dp", "ctx", None),
            P("dp", "ctx", None),
            P("dp", "ctx", None),
            P("dp", None, "ctx"),
            P("dp", "ctx", None),
            P("dp", None),
            P("dp", None),
            P("dp", None, None),
        ),
        out_specs=(
            P("dp", "ctx", None),
            P("dp", "ctx", None),
            P("dp", "ctx", None),
            P(("dp", "ctx"), None),
        ),
        check_vma=False,
    )
```

```python
import functools
import math

import jax
import jax.numpy as jnp
from jax import lax
from jax.experimental import pallas as pl
from jax.experimental.pallas import tpu as pltpu
from jax.sharding import PartitionSpec as P

bf16 = jnp.bfloat16
f32 = jnp.float32
i32 = jnp.int32
QH, KVH, DH, BLOCK = 48, 4, 128, 128
GS = QH // KVH
GW = GS * DH
NZ = 8
TOK = 2 * NZ * BLOCK
MANY = 4
SCALE = 1.0 / math.sqrt(DH)
LOG2E = math.log2(math.e)
SMEM = pl.BlockSpec(memory_space=pltpu.SMEM)
VMEM = pl.BlockSpec(memory_space=pltpu.VMEM)
PARAMS = pltpu.CompilerParams(vmem_limit_bytes=60 << 20)
SIZES = (256, 256, 256, 256, 128, 128, 256, 256, 256)


def dot(a, b):
    return jnp.dot(a, b, preferred_element_type=f32)


def move(value, to):
    pairs = []
    for xh in range(2):
        for y in range(4):
            for c in range(2):
                for z in range(NZ):
                    for xl in range(2):
                        h2, y2, c2, z2, x2 = to(xh, y, c, z, xl)
                        flat = lambda a, b, d, e, f: ((a * 4 + b) * 2 + d) * 16 + e * 2 + f
                        pairs.append((flat(xh, y, c, z, xl), flat(h2, y2, c2, z2, x2)))
    return lax.ppermute(value, ("dp", "ctx"), [p for p in pairs if p[0] != p[1]])


def along_z(value, steps):
    return move(value, lambda h, y, c, z, x: (h, y, c, (z + steps) % NZ, x))


def moved0(value):
    return move(value, lambda h, y, c, z, x: (h, y, x, z, c))


def out0(value):
    stays = lax.axis_index("dp") % 2 == lax.axis_index("ctx") % 2
    return jnp.where(stays, value, moved0(value))


def out1(value):
    return move(value, lambda h, y, c, z, x: (h, y, 1 - x, z, c))


def back0(value):
    return out0(value)


def back1(value):
    return move(value, lambda h, y, c, z, x: (h, y, x, z, 1 - c))


def vis_kernel(place_ref, tree_ref, out_ref, anc_ref):
    z, core = place_ref[0], place_ref[2]
    for s in range(2):

        def clear(i, c):
            anc_ref[i] = 0
            out_ref[s, i] = 0
            return c

        lax.fori_loop(0, 16, clear, 0)

        def climb(i, b):
            anc_ref[b] = 1
            return tree_ref[0, b]

        lax.fori_loop(0, 16, climb, tree_ref[1, z * 2 + (core + s) % 2])
        out_ref[s, 0] = s

        def put(r, n):
            u = lax.rem(z + r // 2, NZ) * 2 + (core + r) % 2
            hit = jnp.where(r == s, 0, anc_ref[tree_ref[1, u]])

            @pl.when(hit == 1)
            def _():
                out_ref[s, n] = r

            return n + hit

        out_ref[s, 16] = lax.fori_loop(0, 16, put, 1)


def visible_lists(place, tree):
    return pl.pallas_call(
        vis_kernel,
        out_shape=jax.ShapeDtypeStruct((2, 17), i32),
        in_specs=[SMEM] * 2,
        out_specs=SMEM,
        scratch_shapes=[pltpu.SMEM((16,), i32)],
        name="visible_lists",
    )(place, tree)


def pieces(v):
    a = v.astype(bf16)
    v = v - a.astype(f32)
    b = v.astype(bf16)
    return a, b, (v - b.astype(f32)).astype(bf16)


def prep_kernel(turn, place_ref, q_ref, do_ref, o_ref, l_ref, *refs):
    out_ref = refs[-1]
    if turn == 0:
        x_ref, xs_ref, out_ref = refs
        n = xs_ref.shape[2]
        for k in range(4):
            xs_ref[k] = x_ref[:, k * n : (k + 1) * n]
    first = (((place_ref[1] + turn) % 2) * 2 + pl.program_id(0)) * GS
    pos = place_ref[3] + lax.broadcasted_iota(i32, (BLOCK, DH), 0)
    inside = jnp.zeros((BLOCK, DH), jnp.bool_)
    for m in range(8):
        inside = inside | ((pos >= place_ref[5 + 2 * m]) & (pos < place_ref[6 + 2 * m]))
    scored = jnp.where(inside, 0.0, 1.0)
    out_ref[:BLOCK, :GW] = q_ref[...]
    zero = jnp.zeros((16 - 6, DH), bf16)
    for h in range(GS):
        c = slice(h * DH, (h + 1) * DH)
        g = do_ref[:, c].astype(f32) * scored
        out_ref[:BLOCK, GW + h * DH : GW + (h + 1) * DH] = g.astype(bf16)
        logs = pieces(l_ref[pl.ds(first + h, 1), :] * LOG2E)
        dots = pieces(jnp.sum((g * o_ref[:, c].astype(f32)).T, axis=0, keepdims=True))
        out_ref[BLOCK:, c] = jnp.concatenate([*logs, *dots, zero], 0)
        out_ref[BLOCK:, GW + h * DH : GW + (h + 1) * DH] = jnp.zeros((16, DH), bf16)


def prep(place, q, do, o, logs, turn, x=None):
    half = lambda i, p: ((p[1] + turn) % 2) * 2 + i
    nat = pl.BlockSpec((BLOCK, GW), lambda i, p: (0, half(i, p)))
    ins, args = [nat, nat, nat, pl.BlockSpec((QH, BLOCK), lambda i, p: (0, 0))], [q, do, o, logs]
    outs = [pl.BlockSpec((BLOCK + 16, 2 * GW), lambda i, p: (0, i))]
    shapes = [jax.ShapeDtypeStruct((BLOCK + 16, 4 * GW), bf16)]
    if x is not None:
        n = x.shape[1] // 8
        ins, args = ins + [pl.BlockSpec((BLOCK, 4 * n), lambda i, p: (0, i))], args + [x]
        outs = [pl.BlockSpec((4, BLOCK, n), lambda i, p: (i, 0, 0))] + outs
        shapes = [jax.ShapeDtypeStruct((8, BLOCK, n), bf16)] + shapes
    return pl.pallas_call(
        functools.partial(prep_kernel, turn),
        grid_spec=pltpu.PrefetchScalarGridSpec(num_scalar_prefetch=1, grid=(2,), in_specs=ins, out_specs=outs),
        out_shape=shapes,
        compiler_params=PARAMS,
        cost_estimate=pl.CostEstimate(flops=10**6, bytes_accessed=3 * 10**6, transcendentals=0),
        name="prep",
    )(place, *args)


def row_of(q_ref, at):
    p = q_ref[BLOCK:, :].astype(f32)
    return p[at : at + 1] + p[at + 1 : at + 2] + p[at + 2 : at + 3]


def over_visible(vis_ref, s, part):
    n = vis_ref[s, 16] - 1
    part([s], True)

    def body(i, c):
        part([vis_ref[s, 1 + MANY * i + k] for k in range(MANY)], False)
        return c

    lax.fori_loop(0, n // MANY, body, 0)
    left = MANY // 2
    while left:
        at = 1 + n // (2 * left) * (2 * left)

        @pl.when(n // left % 2 == 1)
        def _():
            part([vis_ref[s, at + k] for k in range(left)], False)

        left //= 2


def rows(blk):
    return pl.ds(pl.multiple_of(blk * BLOCK, BLOCK), BLOCK)


def taken(ref, blocks):
    return jnp.concatenate([ref[rows(b), :] for b in blocks], 0)


def added(ref, blocks, v):
    for i, b in enumerate(blocks):
        ref[rows(b), :] += v[i * BLOCK : (i + 1) * BLOCK]


def fill(held, parts):
    at = 0
    for p in parts:
        n = p.shape[0]
        held[at : at + n, :] = p[...]
        at += n


def spill(held, parts):
    at = 0
    for p in parts:
        n = p.shape[0]
        p[:, -DH:] = held[at : at + n, :].astype(bf16)
        at += n


def masked_if(diag, p):
    if not diag:
        return p
    k = lax.broadcasted_iota(i32, p.shape, 0)
    q = lax.broadcasted_iota(i32, p.shape, 1) % BLOCK
    return jnp.where(k <= q, p, 0.0)


def setup_kernel(turn, place_ref, *refs):
    t_ref, n_ref, r_ref = refs[-3:]
    q, g = refs[0][...], refs[1][...]
    if turn == 0:
        stays = place_ref[1] == place_ref[2]
        q, g = jnp.where(stays, refs[2][...], q), jnp.where(stays, refs[3][...], g)
    for i, v in enumerate((q, g)):
        for h in range(GS):
            c = slice(h * DH, (h + 1) * DH)
            t_ref[0, i * DH : (i + 1) * DH, c] = v[:BLOCK, c].T
            n_ref[0, i * GW + h * DH : i * GW + (h + 1) * DH, :] = v[:BLOCK, c]
    r_ref[0, 0:1, :] = row_of(q, 0)
    r_ref[0, 1:2, :] = row_of(q, 3)


def setup(place, turn, *given):
    nat = [pl.BlockSpec((BLOCK + 16, GW), lambda i, p, k=k: (0, 2 * i + k)) for k in range(2)]
    shapes = [((2 * DH, GW), bf16), ((2 * GW, DH), bf16), ((2, GW), f32)]
    return pl.pallas_call(
        functools.partial(setup_kernel, turn),
        grid_spec=pltpu.PrefetchScalarGridSpec(
            num_scalar_prefetch=1,
            grid=(2,),
            in_specs=nat * len(given),
            out_specs=[pl.BlockSpec((1, *n), lambda i, p: (i, 0, 0)) for n, _ in shapes],
        ),
        out_shape=[jax.ShapeDtypeStruct((2, *n), t) for n, t in shapes],
        compiler_params=PARAMS,
        cost_estimate=pl.CostEstimate(flops=10**6, bytes_accessed=5 * 10**6, transcendentals=0),
        name="setup",
    )(place, *[v for v in given for _ in range(2)])


def value_kernel(vis_ref, *refs):
    np_ = len(SIZES)
    slots, refs = (refs[:3], refs[3:6]), refs[6:]
    ks, outs = refs[:np_], refs[np_ : 2 * np_]
    k_all, dv_all, p_buf = refs[2 * np_ :]
    fill(k_all, ks)
    dv_all[...] = jnp.zeros_like(dv_all)
    for s, (t_ref, n_ref, r_ref) in enumerate(slots):

        def part(blocks, diag, t_ref=t_ref, n_ref=n_ref, r_ref=r_ref):
            k, n = taken(k_all, blocks), len(blocks) * BLOCK
            p = jnp.exp2(dot(k, t_ref[0]) * (SCALE * LOG2E) - r_ref[0, 0:1, :])
            p_buf[:n, :] = masked_if(diag, p).astype(bf16)
            added(dv_all, blocks, dot(p_buf[:n, :], n_ref[0]))

        over_visible(vis_ref, s, part)
    spill(dv_all, outs)


def value_pass(vis, ready, kvs):
    part = [pl.BlockSpec((n, DH), lambda i, v: (0, i)) for n in SIZES]
    return pl.pallas_call(
        value_kernel,
        grid_spec=pltpu.PrefetchScalarGridSpec(
            num_scalar_prefetch=1,
            grid=(2,),
            in_specs=[
                pl.BlockSpec((1, DH, GW), lambda i, v: (i, 0, 0)),
                pl.BlockSpec((1, GW, DH), lambda i, v: (i, 1, 0)),
                pl.BlockSpec((1, 2, GW), lambda i, v: (i, 0, 0)),
            ]
            * 2
            + part,
            out_specs=part,
            scratch_shapes=[
                pltpu.VMEM((TOK, DH), bf16),
                pltpu.VMEM((TOK, DH), f32),
                pltpu.VMEM((MANY * BLOCK, GW), bf16),
            ],
        ),
        out_shape=[jax.ShapeDtypeStruct((n, 2 * DH), bf16) for n in SIZES],
        compiler_params=PARAMS,
        cost_estimate=pl.CostEstimate(flops=8 * 10**9, bytes_accessed=8 * 10**6, transcendentals=6 * 10**6),
        name="value_pass",
    )(vis, *ready, *kvs)


def key_kernel(vis_ref, *refs):
    np_ = len(SIZES)
    slots, refs = (refs[:3], refs[3:6]), refs[6:]
    ks, vs, refs = refs[:np_], refs[np_ : 2 * np_], refs[2 * np_ :]
    others = refs[: -np_ - 7]
    at = GW if others else 0
    dqs, outs = refs[-np_ - 7 : -np_ - 5], refs[-np_ - 5 : -5]
    k_all, v_all, dk_all, s_buf, dqt = refs[-5:]
    fill(k_all, ks)
    fill(v_all, vs)
    dk_all[...] = jnp.zeros_like(dk_all)
    for s, (t_ref, n_ref, r_ref) in enumerate(slots):
        dqt[...] = jnp.zeros_like(dqt)

        def part(blocks, diag, t_ref=t_ref, n_ref=n_ref, r_ref=r_ref):
            k, v, n = taken(k_all, blocks), taken(v_all, blocks), len(blocks) * BLOCK
            logs = r_ref[0, 0:1, :] - math.log2(SCALE)
            p = jnp.exp2(dot(k, t_ref[0, :DH, :]) * (SCALE * LOG2E) - logs)
            d = dot(v, t_ref[0, DH:, :]) - r_ref[0, 1:2, :]
            s_buf[:n, :] = (masked_if(diag, p) * d).astype(bf16)
            dqt[...] += dot(k.T, s_buf[:n, :])
            added(dk_all, blocks, dot(s_buf[:n, :], n_ref[0]))

        over_visible(vis_ref, s, part)
        for h in range(GS):
            c = slice(h * DH, (h + 1) * DH)
            dqs[s][:, at + h * DH : at + (h + 1) * DH] = dqt[:, c].T.astype(bf16)
    spill(dk_all, outs)
    for o, p in zip(dqs, others):
        o[:, :at] = p[...]
    for o, p in zip(outs, others[2:]):
        o[:, :DH] = p[...]


def key_pass(vis, group, ready, kvs, others=()):
    part = [pl.BlockSpec((n, DH), lambda i, v, k=k: (0, group + 2 * k)) for k in range(2) for n in SIZES]
    whole = lambda shape: pl.BlockSpec(shape, lambda i, v: (0, 0))
    dq = [jax.ShapeDtypeStruct((BLOCK, (group + 1) * GW), bf16)] * 2
    dk = [jax.ShapeDtypeStruct((n, (group + 1) * DH), bf16) for n in SIZES]
    out = pl.pallas_call(
        key_kernel,
        grid_spec=pltpu.PrefetchScalarGridSpec(
            num_scalar_prefetch=1,
            grid=(1,),
            in_specs=[
                pl.BlockSpec((1, 2 * DH, GW), lambda i, v: (group, 0, 0)),
                pl.BlockSpec((1, GW, DH), lambda i, v: (group, 0, 0)),
                pl.BlockSpec((1, 2, GW), lambda i, v: (group, 0, 0)),
            ]
            * 2
            + part
            + [whole(m.shape) for m in others],
            out_specs=[whole(d.shape) for d in dq + dk],
            scratch_shapes=[
                pltpu.VMEM((TOK, DH), bf16),
                pltpu.VMEM((TOK, DH), bf16),
                pltpu.VMEM((TOK, DH), f32),
                pltpu.VMEM((MANY * BLOCK, GW), bf16),
                pltpu.VMEM((DH, GW), f32),
            ],
        ),
        out_shape=dq + dk,
        compiler_params=PARAMS,
        cost_estimate=pl.CostEstimate(flops=8 * 10**9, bytes_accessed=8 * 10**6, transcendentals=4 * 10**6),
        name="key_pass",
    )(vis, *ready, *kvs, *kvs, *others)
    return out[:2], out[2:]


def weight_kernel(place_ref, x_ref, *refs):
    np_ = len(refs) - 5
    vgs = refs[:np_]
    keep_ref, give_ref, vg_all, vg_t, x_all = refs[np_:]
    core, y = place_ref[2], place_ref[4]
    fill(vg_all, vgs)
    for i in range(8):
        at = slice(i * BLOCK, (i + 1) * BLOCK)
        x_all[at, :] = x_ref[lax.rem(y + i // 2, 4) * 2 + (core + i) % 2]
        vg_t[:, at] = vg_all[at, :].T
    n = vg_t.shape[0]
    i = lax.broadcasted_iota(i32, (n, n), 0)
    bits = lambda k, m: lax.shift_right_logical(i, k) & m
    row = bits(7, 1) * 256 + bits(1, 7) * 32 + bits(4, 7) * 4 + (bits(8, 1) ^ place_ref[1]) * 2 + bits(0, 1)
    order = jnp.where(row == lax.broadcasted_iota(i32, (n, n), 1), 1.0, 0.0).astype(bf16)
    turned_rows = dot(order, vg_t[...]).astype(bf16)
    w = dot(turned_rows, x_all[...]) * (1.0 / 16.0)
    keep_ref[...] = w[: n // 2]
    give_ref[...] = w[n // 2 :].astype(bf16)


def weight_part(place, x, vgs):
    tot = 8 * BLOCK
    n, cols = vgs[0].shape[1], x.shape[2]
    return pl.pallas_call(
        weight_kernel,
        in_specs=[SMEM] + [VMEM] * (len(vgs) + 1),
        out_specs=[VMEM] * 2,
        out_shape=[jax.ShapeDtypeStruct((n // 2, cols), t) for t in (f32, bf16)],
        scratch_shapes=[pltpu.VMEM((tot, n), bf16), pltpu.VMEM((n, tot), bf16), pltpu.VMEM((tot, cols), bf16)],
        compiler_params=PARAMS,
        cost_estimate=pl.CostEstimate(flops=10**9, bytes_accessed=4 * 10**6, transcendentals=0),
        name="weight_part",
    )(place, x, *vgs)


def along_y(value, steps):
    return move(value, lambda h, y, c, z, x: (h, (y + steps) % 4, c, z, x))


def other_core(value):
    return move(value, lambda h, y, c, z, x: (h, y, 1 - c, z, x))


def other_x(value):
    return move(value, lambda h, y, c, z, x: (h, y, c, z, 1 - x))


def dealt(value, members):
    return lax.all_to_all(value, ("dp", "ctx"), 0, 0, axis_index_groups=members, tiled=True)


def device(xh, y, c, z, xl):
    return ((xh * 4 + y) * 2 + c) * 16 + z * 2 + xl


OVER_Y = [
    [device(h, y, c, z, x) for y in range(4) for c in range(2)] for h in range(2) for z in range(NZ) for x in range(2)
]
OVER_Z = [
    [device(h, y, c, z, x) for h in range(2) for z in range(NZ)] for y in range(4) for c in range(2) for x in range(2)
]


def near(own):
    return along_z(own, 2), along_z(own, -2), along_z(own, 1), along_z(own, -1)


def far(own, got):
    a2, b2, a1, b1 = got
    h = own.shape[0] // 2
    a3, b3 = along_z(a2, 1), along_z(b2, -1)
    a4, b4 = along_z(a2[:h], 2), along_z(b2[h:], -2)
    return [own, b1, b2, b3, a4, b4, a3, a2, a1]


def wide(v):
    return v.astype(f32)


def reduce_far(parts):
    p0, p1, p2, p3, p4a, p4b, p5, p6, p7 = parts
    return along_z(p3, 1), along_z(p5, -1), along_z(p4a, 2), along_z(p4b, -2), along_z(p1, 1), along_z(p7, -1)


def reduce_near(parts, got):
    p2, p6 = parts[2], parts[7]
    a, b, c, d = got[:4]
    h = c.shape[0]
    zero = jnp.zeros_like(c, f32)
    u = wide(p2) + wide(a) + jnp.concatenate([wide(c), zero], 0)
    v = wide(p6) + wide(b) + jnp.concatenate([zero, wide(d)], 0)
    return along_z(u.astype(bf16), 2), along_z(v.astype(bf16), -2)


def reduce_end(parts, got, last):
    total = wide(parts[0]) + wide(got[4]) + wide(got[5]) + wide(last[0]) + wide(last[1])
    return total.astype(bf16)


def home(value, xl):
    h = value.shape[0] // 2
    a, b = back0(value[:h]), back1(value[h:])
    return jnp.where(xl == 0, jnp.concatenate([a, b], 1), jnp.concatenate([b, a], 1))


def tie(*values):
    return lax.optimization_barrier(values)


def local(
    queries, keys, values, saved_output, output_grad, log_sums, layer_input, parents, placement, tool_spans
):
    ctx, dp = lax.axis_index("ctx"), lax.axis_index("dp")
    z, xl = ctx // 2, ctx % 2
    core, y = dp % 2, dp // 2 % 4
    place = jnp.concatenate([jnp.stack([z, xl, core, ctx * BLOCK, y]).astype(i32), tool_spans[0].reshape(16)])
    half = lambda v, t: lax.dynamic_slice_in_dim(v, ((xl + t) % 2) * 2 * DH, 2 * DH, 1)
    kv = [jnp.concatenate([half(keys[0], t), half(values[0], t)], 1) for t in range(2)]
    tree = jnp.concatenate([parents, placement], 0)
    place, kv, tree = tie(place, kv, tree)
    tree = out0(tree)
    kv = jnp.concatenate([out0(kv[0]), out1(kv[1])], 0)
    arrays = (queries[0], output_grad[0], saved_output[0], log_sums[0])
    (qg1,) = prep(place, *arrays, 1)
    qg1, kv, tree, after = tie(qg1, kv, tree, place)
    moved1 = out1(qg1)
    x, qg0 = prep(after, *arrays, 0, layer_input[0])
    qg0, kv, x = tie(qg0, kv, x)
    early = moved0(qg0)
    kv_near = near(kv)
    vis = visible_lists(after, tree)
    kv_near, x, vis = tie(kv_near, x, vis)
    kvs = far(kv, kv_near)
    x = dealt(x, OVER_Y)
    ready = (*setup(place, 0, early, qg0), *setup(place, 1, moved1))
    kvs, ready, vis, x = tie(kvs, ready, vis, x)

    dvs = value_pass(vis, ready, kvs)
    got = reduce_far(dvs)
    ready, dvs = tie(ready, dvs)
    dq0, dk0 = key_pass(vis, 0, ready, kvs)
    got, dk0, dq0 = tie(got, dk0, dq0)
    last = reduce_near(dvs, got)
    dq1, dks = key_pass(vis, 1, ready, kvs, (*dq0, *dk0))
    last, dks, dq1 = tie(last, dks, dq1)
    value_grad = home(reduce_end(dvs, got, last), xl)
    value_grad, dq1 = tie(value_grad, dq1)
    pair = jnp.concatenate([value_grad, other_core(value_grad)], 0)
    dq1 = [back0(dq1[0]), back1(dq1[1])]
    y1, y3 = along_y(pair, -1), along_y(pair, 1)
    y1, y3, dks = tie(y1, y3, dks)
    vgs = [pair, y1, along_y(y3[:BLOCK], 1), along_y(y1[BLOCK:], -1), y3]
    dk_got = reduce_far(dks)
    vgs, dq1 = tie(vgs, dq1)
    keep, give = weight_part(place, x, vgs)
    give, dk_got = tie(give, dk_got)
    w = (keep + wide(other_x(give))).astype(bf16)
    cols = w.shape[1]
    dk_last = reduce_near(dks, dk_got)
    w, dk_last = tie(w, dk_last)
    w = dealt(w.reshape(16, 16, cols), OVER_Z)
    key_grad = home(reduce_end(dks, dk_got, dk_last), xl)
    w = dealt(jnp.sum(wide(w), 0).reshape(8, 2, cols), OVER_Y)
    weight_grad = jnp.transpose(w, (1, 0, 2)).reshape(2, 8 * cols)
    query_grad = jnp.where(xl == 0, jnp.concatenate(dq1, 1), jnp.concatenate(dq1[::-1], 1))
    return (query_grad[None], key_grad[None], value_grad[None], weight_grad)


def solution(mesh):
    return jax.shard_map(
        local,
        mesh=mesh,
        in_specs=(
            P("dp", "ctx", None),
            P("dp", "ctx", None),
            P("dp", "ctx", None),
            P("dp", "ctx", None),
            P("dp", "ctx", None),
            P("dp", None, "ctx"),
            P("dp", "ctx", None),
            P("dp", None),
            P("dp", None),
            P("dp", None, None),
        ),
        out_specs=(
            P("dp", "ctx", None),
            P("dp", "ctx", None),
            P("dp", "ctx", None),
            P(("dp", "ctx"), None),
        ),
        check_vma=False,
    )
```

```python
import functools
import math

import jax
import jax.numpy as jnp
from jax import lax
from jax.experimental import pallas as pl
from jax.experimental.pallas import tpu as pltpu
from jax.sharding import PartitionSpec as P

bf16 = jnp.bfloat16
f32 = jnp.float32
i32 = jnp.int32
QH, KVH, DH, BLOCK = 48, 4, 128, 128
GS = QH // KVH
GW = GS * DH
NZ = 8
TOK = 2 * NZ * BLOCK
MANY = 4
SCALE = 1.0 / math.sqrt(DH)
LOG2E = math.log2(math.e)
SMEM = pl.BlockSpec(memory_space=pltpu.SMEM)
VMEM = pl.BlockSpec(memory_space=pltpu.VMEM)
PARAMS = pltpu.CompilerParams(vmem_limit_bytes=60 << 20)
SIZES = (256, 256, 256, 256, 128, 128, 256, 256, 256)


def dot(a, b):
    return jnp.dot(a, b, preferred_element_type=f32)


def move(value, to):
    pairs = []
    for xh in range(2):
        for y in range(4):
            for c in range(2):
                for z in range(NZ):
                    for xl in range(2):
                        h2, y2, c2, z2, x2 = to(xh, y, c, z, xl)
                        flat = lambda a, b, d, e, f: ((a * 4 + b) * 2 + d) * 16 + e * 2 + f
                        pairs.append((flat(xh, y, c, z, xl), flat(h2, y2, c2, z2, x2)))
    return lax.ppermute(value, ("dp", "ctx"), [p for p in pairs if p[0] != p[1]])


def along_z(value, steps):
    return move(value, lambda h, y, c, z, x: (h, y, c, (z + steps) % NZ, x))


def moved0(value):
    return move(value, lambda h, y, c, z, x: (h, y, x, z, c))


def out0(value):
    stays = lax.axis_index("dp") % 2 == lax.axis_index("ctx") % 2
    return jnp.where(stays, value, moved0(value))


def out1(value):
    return move(value, lambda h, y, c, z, x: (h, y, 1 - x, z, c))


def back0(value):
    return out0(value)


def back1(value):
    return move(value, lambda h, y, c, z, x: (h, y, x, z, 1 - c))


def vis_kernel(place_ref, tree_ref, out_ref, anc_ref):
    z, core = place_ref[0], place_ref[2]
    for s in range(2):

        def clear(i, c):
            anc_ref[i] = 0
            out_ref[s, i] = 0
            return c

        lax.fori_loop(0, 16, clear, 0)

        def climb(i, b):
            anc_ref[b] = 1
            return tree_ref[0, b]

        lax.fori_loop(0, 16, climb, tree_ref[1, z * 2 + (core + s) % 2])
        out_ref[s, 0] = s

        def put(r, n):
            u = lax.rem(z + r // 2, NZ) * 2 + (core + r) % 2
            hit = jnp.where(r == s, 0, anc_ref[tree_ref[1, u]])

            @pl.when(hit == 1)
            def _():
                out_ref[s, n] = r

            return n + hit

        out_ref[s, 16] = lax.fori_loop(0, 16, put, 1)


def visible_lists(place, tree):
    return pl.pallas_call(
        vis_kernel,
        out_shape=jax.ShapeDtypeStruct((2, 17), i32),
        in_specs=[SMEM] * 2,
        out_specs=SMEM,
        scratch_shapes=[pltpu.SMEM((16,), i32)],
        name="visible_lists",
    )(place, tree)


def pieces(v):
    a = v.astype(bf16)
    v = v - a.astype(f32)
    b = v.astype(bf16)
    return a, b, (v - b.astype(f32)).astype(bf16)


def prep_kernel(turn, place_ref, q_ref, do_ref, o_ref, l_ref, *refs):
    out_ref = refs[-1]
    if turn == 0:
        x_ref, xs_ref, out_ref = refs
        n = xs_ref.shape[2]
        for k in range(4):
            xs_ref[k] = x_ref[:, k * n : (k + 1) * n]
    first = (((place_ref[1] + turn) % 2) * 2 + pl.program_id(0)) * GS
    pos = place_ref[3] + lax.broadcasted_iota(i32, (BLOCK, DH), 0)
    inside = jnp.zeros((BLOCK, DH), jnp.bool_)
    for m in range(8):
        inside = inside | ((pos >= place_ref[5 + 2 * m]) & (pos < place_ref[6 + 2 * m]))
    scored = jnp.where(inside, 0.0, 1.0)
    out_ref[:BLOCK, :GW] = q_ref[...]
    zero = jnp.zeros((16 - 6, DH), bf16)
    for h in range(GS):
        c = slice(h * DH, (h + 1) * DH)
        g = do_ref[:, c].astype(f32) * scored
        out_ref[:BLOCK, GW + h * DH : GW + (h + 1) * DH] = g.astype(bf16)
        logs = pieces(l_ref[pl.ds(first + h, 1), :] * LOG2E)
        dots = pieces(jnp.sum((g * o_ref[:, c].astype(f32)).T, axis=0, keepdims=True))
        out_ref[BLOCK:, c] = jnp.concatenate([*logs, *dots, zero], 0)
        out_ref[BLOCK:, GW + h * DH : GW + (h + 1) * DH] = jnp.zeros((16, DH), bf16)


def prep(place, q, do, o, logs, turn, x=None):
    half = lambda i, p: ((p[1] + turn) % 2) * 2 + i
    nat = pl.BlockSpec((BLOCK, GW), lambda i, p: (0, half(i, p)))
    ins, args = [nat, nat, nat, pl.BlockSpec((QH, BLOCK), lambda i, p: (0, 0))], [q, do, o, logs]
    outs = [pl.BlockSpec((BLOCK + 16, 2 * GW), lambda i, p: (0, i))]
    shapes = [jax.ShapeDtypeStruct((BLOCK + 16, 4 * GW), bf16)]
    if x is not None:
        n = x.shape[1] // 8
        ins, args = ins + [pl.BlockSpec((BLOCK, 4 * n), lambda i, p: (0, i))], args + [x]
        outs = [pl.BlockSpec((4, BLOCK, n), lambda i, p: (i, 0, 0))] + outs
        shapes = [jax.ShapeDtypeStruct((8, BLOCK, n), bf16)] + shapes
    return pl.pallas_call(
        functools.partial(prep_kernel, turn),
        grid_spec=pltpu.PrefetchScalarGridSpec(num_scalar_prefetch=1, grid=(2,), in_specs=ins, out_specs=outs),
        out_shape=shapes,
        compiler_params=PARAMS,
        cost_estimate=pl.CostEstimate(flops=10**6, bytes_accessed=3 * 10**6, transcendentals=0),
        name="prep",
    )(place, *args)


def row_of(q_ref, at):
    p = q_ref[BLOCK:, :].astype(f32)
    return p[at : at + 1] + p[at + 1 : at + 2] + p[at + 2 : at + 3]


def over_visible(vis_ref, s, part):
    n = vis_ref[s, 16] - 1
    part([s], True)

    def body(i, c):
        part([vis_ref[s, 1 + MANY * i + k] for k in range(MANY)], False)
        return c

    lax.fori_loop(0, n // MANY, body, 0)
    left = MANY // 2
    while left:
        at = 1 + n // (2 * left) * (2 * left)

        @pl.when(n // left % 2 == 1)
        def _():
            part([vis_ref[s, at + k] for k in range(left)], False)

        left //= 2


def rows(blk):
    return pl.ds(pl.multiple_of(blk * BLOCK, BLOCK), BLOCK)


def taken(ref, blocks):
    return jnp.concatenate([ref[rows(b), :] for b in blocks], 0)


def added(ref, blocks, v):
    for i, b in enumerate(blocks):
        ref[rows(b), :] += v[i * BLOCK : (i + 1) * BLOCK]


def fill(held, parts):
    at = 0
    for p in parts:
        n = p.shape[0]
        held[at : at + n, :] = p[...]
        at += n


def spill(held, parts):
    at = 0
    for p in parts:
        n = p.shape[0]
        p[:, -DH:] = held[at : at + n, :].astype(bf16)
        at += n


def masked_if(diag, p):
    if not diag:
        return p
    k = lax.broadcasted_iota(i32, p.shape, 0)
    q = lax.broadcasted_iota(i32, p.shape, 1) % BLOCK
    return jnp.where(k <= q, p, 0.0)


def setup_kernel(turn, place_ref, *refs):
    t_ref, n_ref, r_ref = refs[-3:]
    q, g = refs[0][...], refs[1][...]
    if turn == 0:
        stays = place_ref[1] == place_ref[2]
        q, g = jnp.where(stays, refs[2][...], q), jnp.where(stays, refs[3][...], g)
    for i, v in enumerate((q, g)):
        for h in range(GS):
            c = slice(h * DH, (h + 1) * DH)
            t_ref[0, i * DH : (i + 1) * DH, c] = v[:BLOCK, c].T
            n_ref[0, i * GW + h * DH : i * GW + (h + 1) * DH, :] = v[:BLOCK, c]
    r_ref[0, 0:1, :] = row_of(q, 0)
    r_ref[0, 1:2, :] = row_of(q, 3)


def setup(place, turn, *given):
    nat = [pl.BlockSpec((BLOCK + 16, GW), lambda i, p, k=k: (0, 2 * i + k)) for k in range(2)]
    shapes = [((2 * DH, GW), bf16), ((2 * GW, DH), bf16), ((2, GW), f32)]
    return pl.pallas_call(
        functools.partial(setup_kernel, turn),
        grid_spec=pltpu.PrefetchScalarGridSpec(
            num_scalar_prefetch=1,
            grid=(2,),
            in_specs=nat * len(given),
            out_specs=[pl.BlockSpec((1, *n), lambda i, p: (i, 0, 0)) for n, _ in shapes],
        ),
        out_shape=[jax.ShapeDtypeStruct((2, *n), t) for n, t in shapes],
        compiler_params=PARAMS,
        cost_estimate=pl.CostEstimate(flops=10**6, bytes_accessed=5 * 10**6, transcendentals=0),
        name="setup",
    )(place, *[v for v in given for _ in range(2)])


def value_kernel(vis_ref, *refs):
    np_ = len(SIZES)
    slots, refs = (refs[:3], refs[3:6]), refs[6:]
    ks, outs = refs[:np_], refs[np_ : 2 * np_]
    k_all, dv_all, p_buf = refs[2 * np_ :]
    fill(k_all, ks)
    dv_all[...] = jnp.zeros_like(dv_all)
    for s, (t_ref, n_ref, r_ref) in enumerate(slots):

        def part(blocks, diag, t_ref=t_ref, n_ref=n_ref, r_ref=r_ref):
            k, n = taken(k_all, blocks), len(blocks) * BLOCK
            p = jnp.exp2(dot(k, t_ref[0]) * (SCALE * LOG2E) - r_ref[0, 0:1, :])
            p_buf[:n, :] = masked_if(diag, p).astype(bf16)
            added(dv_all, blocks, dot(p_buf[:n, :], n_ref[0]))

        over_visible(vis_ref, s, part)
    spill(dv_all, outs)


def value_pass(vis, ready, kvs):
    part = [pl.BlockSpec((n, DH), lambda i, v: (0, i)) for n in SIZES]
    return pl.pallas_call(
        value_kernel,
        grid_spec=pltpu.PrefetchScalarGridSpec(
            num_scalar_prefetch=1,
            grid=(2,),
            in_specs=[
                pl.BlockSpec((1, DH, GW), lambda i, v: (i, 0, 0)),
                pl.BlockSpec((1, GW, DH), lambda i, v: (i, 1, 0)),
                pl.BlockSpec((1, 2, GW), lambda i, v: (i, 0, 0)),
            ]
            * 2
            + part,
            out_specs=part,
            scratch_shapes=[
                pltpu.VMEM((TOK, DH), bf16),
                pltpu.VMEM((TOK, DH), f32),
                pltpu.VMEM((MANY * BLOCK, GW), bf16),
            ],
        ),
        out_shape=[jax.ShapeDtypeStruct((n, 2 * DH), bf16) for n in SIZES],
        compiler_params=PARAMS,
        cost_estimate=pl.CostEstimate(flops=8 * 10**9, bytes_accessed=8 * 10**6, transcendentals=6 * 10**6),
        name="value_pass",
    )(vis, *ready, *kvs)


def key_kernel(vis_ref, *refs):
    np_ = len(SIZES)
    slots, refs = (refs[:3], refs[3:6]), refs[6:]
    ks, vs, refs = refs[:np_], refs[np_ : 2 * np_], refs[2 * np_ :]
    others = refs[: -np_ - 7]
    at = GW if others else 0
    dqs, outs = refs[-np_ - 7 : -np_ - 5], refs[-np_ - 5 : -5]
    k_all, v_all, dk_all, s_buf, dqt = refs[-5:]
    fill(k_all, ks)
    fill(v_all, vs)
    dk_all[...] = jnp.zeros_like(dk_all)
    for s, (t_ref, n_ref, r_ref) in enumerate(slots):
        dqt[...] = jnp.zeros_like(dqt)

        def part(blocks, diag, t_ref=t_ref, n_ref=n_ref, r_ref=r_ref):
            k, v, n = taken(k_all, blocks), taken(v_all, blocks), len(blocks) * BLOCK
            logs = r_ref[0, 0:1, :] - math.log2(SCALE)
            p = jnp.exp2(dot(k, t_ref[0, :DH, :]) * (SCALE * LOG2E) - logs)
            d = dot(v, t_ref[0, DH:, :]) - r_ref[0, 1:2, :]
            s_buf[:n, :] = (masked_if(diag, p) * d).astype(bf16)
            dqt[...] += dot(k.T, s_buf[:n, :])
            added(dk_all, blocks, dot(s_buf[:n, :], n_ref[0]))

        over_visible(vis_ref, s, part)
        for h in range(GS):
            c = slice(h * DH, (h + 1) * DH)
            dqs[s][:, at + h * DH : at + (h + 1) * DH] = dqt[:, c].T.astype(bf16)
    spill(dk_all, outs)
    for o, p in zip(dqs, others):
        o[:, :at] = p[...]
    for o, p in zip(outs, others[2:]):
        o[:, :DH] = p[...]


def key_pass(vis, group, ready, kvs, others=()):
    part = [pl.BlockSpec((n, DH), lambda i, v, k=k: (0, group + 2 * k)) for k in range(2) for n in SIZES]
    whole = lambda shape: pl.BlockSpec(shape, lambda i, v: (0, 0))
    dq = [jax.ShapeDtypeStruct((BLOCK, (group + 1) * GW), bf16)] * 2
    dk = [jax.ShapeDtypeStruct((n, (group + 1) * DH), bf16) for n in SIZES]
    out = pl.pallas_call(
        key_kernel,
        grid_spec=pltpu.PrefetchScalarGridSpec(
            num_scalar_prefetch=1,
            grid=(1,),
            in_specs=[
                pl.BlockSpec((1, 2 * DH, GW), lambda i, v: (group, 0, 0)),
                pl.BlockSpec((1, GW, DH), lambda i, v: (group, 0, 0)),
                pl.BlockSpec((1, 2, GW), lambda i, v: (group, 0, 0)),
            ]
            * 2
            + part
            + [whole(m.shape) for m in others],
            out_specs=[whole(d.shape) for d in dq + dk],
            scratch_shapes=[
                pltpu.VMEM((TOK, DH), bf16),
                pltpu.VMEM((TOK, DH), bf16),
                pltpu.VMEM((TOK, DH), f32),
                pltpu.VMEM((MANY * BLOCK, GW), bf16),
                pltpu.VMEM((DH, GW), f32),
            ],
        ),
        out_shape=dq + dk,
        compiler_params=PARAMS,
        cost_estimate=pl.CostEstimate(flops=8 * 10**9, bytes_accessed=8 * 10**6, transcendentals=4 * 10**6),
        name="key_pass",
    )(vis, *ready, *kvs, *kvs, *others)
    return out[:2], out[2:]


def weight_kernel(place_ref, x_ref, *refs):
    np_ = len(refs) - 5
    vgs = refs[:np_]
    keep_ref, give_ref, vg_all, vg_t, x_all = refs[np_:]
    core, y = place_ref[2], place_ref[4]
    fill(vg_all, vgs)
    for i in range(8):
        at = slice(i * BLOCK, (i + 1) * BLOCK)
        x_all[at, :] = x_ref[lax.rem(y + i // 2, 4) * 2 + (core + i) % 2]
        vg_t[:, at] = vg_all[at, :].T
    n = vg_t.shape[0]
    i = lax.broadcasted_iota(i32, (n, n), 0)
    bits = lambda k, m: lax.shift_right_logical(i, k) & m
    row = bits(7, 1) * 256 + bits(1, 7) * 32 + bits(4, 7) * 4 + (bits(8, 1) ^ place_ref[1]) * 2 + bits(0, 1)
    order = jnp.where(row == lax.broadcasted_iota(i32, (n, n), 1), 1.0, 0.0).astype(bf16)
    turned_rows = dot(order, vg_t[...]).astype(bf16)
    w = dot(turned_rows, x_all[...]) * (1.0 / 16.0)
    keep_ref[...] = w[: n // 2]
    give_ref[...] = w[n // 2 :].astype(bf16)


def weight_part(place, x, vgs):
    tot = 8 * BLOCK
    n, cols = vgs[0].shape[1], x.shape[2]
    return pl.pallas_call(
        weight_kernel,
        in_specs=[SMEM] + [VMEM] * (len(vgs) + 1),
        out_specs=[VMEM] * 2,
        out_shape=[jax.ShapeDtypeStruct((n // 2, cols), t) for t in (f32, bf16)],
        scratch_shapes=[pltpu.VMEM((tot, n), bf16), pltpu.VMEM((n, tot), bf16), pltpu.VMEM((tot, cols), bf16)],
        compiler_params=PARAMS,
        cost_estimate=pl.CostEstimate(flops=10**9, bytes_accessed=4 * 10**6, transcendentals=0),
        name="weight_part",
    )(place, x, *vgs)


def along_y(value, steps):
    return move(value, lambda h, y, c, z, x: (h, (y + steps) % 4, c, z, x))


def other_core(value):
    return move(value, lambda h, y, c, z, x: (h, y, 1 - c, z, x))


def other_x(value):
    return move(value, lambda h, y, c, z, x: (h, y, c, z, 1 - x))


def dealt(value, members):
    return lax.all_to_all(value, ("dp", "ctx"), 0, 0, axis_index_groups=members, tiled=True)


def device(xh, y, c, z, xl):
    return ((xh * 4 + y) * 2 + c) * 16 + z * 2 + xl


OVER_Y = [
    [device(h, y, c, z, x) for y in range(4) for c in range(2)] for h in range(2) for z in range(NZ) for x in range(2)
]
OVER_Z = [
    [device(h, y, c, z, x) for h in range(2) for z in range(NZ)] for y in range(4) for c in range(2) for x in range(2)
]


def near(own):
    return along_z(own, 2), along_z(own, -2), along_z(own, 1), along_z(own, -1)


def far(own, got):
    a2, b2, a1, b1 = got
    h = own.shape[0] // 2
    a3, b3 = along_z(a2, 1), along_z(b2, -1)
    a4, b4 = along_z(a2[:h], 2), along_z(b2[h:], -2)
    return [own, b1, b2, b3, a4, b4, a3, a2, a1]


def wide(v):
    return v.astype(f32)


def reduce_far(parts):
    p0, p1, p2, p3, p4a, p4b, p5, p6, p7 = parts
    return along_z(p3, 1), along_z(p5, -1), along_z(p4a, 2), along_z(p4b, -2), along_z(p1, 1), along_z(p7, -1)


def reduce_near(parts, got):
    p2, p6 = parts[2], parts[7]
    a, b, c, d = got[:4]
    h = c.shape[0]
    zero = jnp.zeros_like(c, f32)
    u = wide(p2) + wide(a) + jnp.concatenate([wide(c), zero], 0)
    v = wide(p6) + wide(b) + jnp.concatenate([zero, wide(d)], 0)
    return along_z(u.astype(bf16), 2), along_z(v.astype(bf16), -2)


def reduce_end(parts, got, last):
    total = wide(parts[0]) + wide(got[4]) + wide(got[5]) + wide(last[0]) + wide(last[1])
    return total.astype(bf16)


def home(value, xl):
    h = value.shape[0] // 2
    a, b = back0(value[:h]), back1(value[h:])
    return jnp.where(xl == 0, jnp.concatenate([a, b], 1), jnp.concatenate([b, a], 1))


def tie(*values):
    return lax.optimization_barrier(values)


def local(
    queries, keys, values, saved_output, output_grad, log_sums, layer_input, parents, placement, tool_spans
):
    ctx, dp = lax.axis_index("ctx"), lax.axis_index("dp")
    z, xl = ctx // 2, ctx % 2
    core, y = dp % 2, dp // 2 % 4
    place = jnp.concatenate([jnp.stack([z, xl, core, ctx * BLOCK, y]).astype(i32), tool_spans[0].reshape(16)])
    half = lambda v, t: lax.dynamic_slice_in_dim(v, ((xl + t) % 2) * 2 * DH, 2 * DH, 1)
    kv = [jnp.concatenate([half(keys[0], t), half(values[0], t)], 1) for t in range(2)]
    tree = jnp.concatenate([parents, placement], 0)
    place, kv, tree = tie(place, kv, tree)
    tree = out0(tree)
    kv = jnp.concatenate([out0(kv[0]), out1(kv[1])], 0)
    arrays = (queries[0], output_grad[0], saved_output[0], log_sums[0])
    (qg1,) = prep(place, *arrays, 1)
    qg1, kv, tree, after = tie(qg1, kv, tree, place)
    moved1 = out1(qg1)
    x, qg0 = prep(after, *arrays, 0, layer_input[0])
    qg0, kv, x = tie(qg0, kv, x)
    early = moved0(qg0)
    kv_near = near(kv)
    vis = visible_lists(after, tree)
    kv_near, x, vis = tie(kv_near, x, vis)
    kvs = far(kv, kv_near)
    x = dealt(x, OVER_Y)
    ready = (*setup(place, 0, early, qg0), *setup(place, 1, moved1))
    kvs, ready, vis, x = tie(kvs, ready, vis, x)

    dvs = value_pass(vis, ready, kvs)
    got = reduce_far(dvs)
    ready, dvs = tie(ready, dvs)
    dq0, dk0 = key_pass(vis, 0, ready, kvs)
    got, dk0, dq0 = tie(got, dk0, dq0)
    last = reduce_near(dvs, got)
    value_grad = home(reduce_end(dvs, got, last), xl)
    pair = jnp.concatenate([value_grad, other_core(value_grad)], 0)
    ready, pair = tie(ready, pair)
    y1, y3 = along_y(pair, -1), along_y(pair, 1)
    dq1, dks = key_pass(vis, 1, ready, kvs, (*dq0, *dk0))
    y1, y3, dks, dq1 = tie(y1, y3, dks, dq1)
    vgs = [pair, y1, along_y(y3[:BLOCK], 1), along_y(y1[BLOCK:], -1), y3]
    dk_got = reduce_far(dks)
    keep, give = weight_part(place, x, vgs)
    give, dq1 = tie(give, dq1)
    w = (keep + wide(other_x(give))).astype(bf16)
    dq1 = [back0(dq1[0]), back1(dq1[1])]
    cols = w.shape[1]
    w, dk_got = tie(w, dk_got)
    dk_last = reduce_near(dks, dk_got)
    w = dealt(w.reshape(16, 16, cols), OVER_Z)
    w, dk_last = tie(w, dk_last)
    key_grad = home(reduce_end(dks, dk_got, dk_last), xl)
    w = dealt(jnp.sum(wide(w), 0).reshape(8, 2, cols), OVER_Y)
    weight_grad = jnp.transpose(w, (1, 0, 2)).reshape(2, 8 * cols)
    query_grad = jnp.where(xl == 0, jnp.concatenate(dq1, 1), jnp.concatenate(dq1[::-1], 1))
    return (query_grad[None], key_grad[None], value_grad[None], weight_grad)


def solution(mesh):
    return jax.shard_map(
        local,
        mesh=mesh,
        in_specs=(
            P("dp", "ctx", None),
            P("dp", "ctx", None),
            P("dp", "ctx", None),
            P("dp", "ctx", None),
            P("dp", "ctx", None),
            P("dp", None, "ctx"),
            P("dp", "ctx", None),
            P("dp", None),
            P("dp", None),
            P("dp", None, None),
        ),
        out_specs=(
            P("dp", "ctx", None),
            P("dp", "ctx", None),
            P("dp", "ctx", None),
            P(("dp", "ctx"), None),
        ),
        check_vma=False,
    )
```
